128 devices in a mesh: ctx: 16 (over x, y), head: 8 (over z, core).
Axes of the slice: x: 4, y: 4, z: 4, core: 2. Of those that a mesh axis runs over, the one named last changes fastest.
Arguments:
- lin_query: bfloat16 [8192, 8192], P('ctx', 'head'), may hold values from -6 to 6
- lin_key: bfloat16 [8192, 8192], P('ctx', 'head'), may hold values from -6 to 6
- lin_value: bfloat16 [8192, 8192], P('ctx', 'head'), may hold values from -61.2 to 61.2
- lin_gate: bfloat16 [8192, 8192], P('ctx', 'head'), may hold values from -6 to 6
- norm_gain: float32 [8192], P('head'), may hold values from 0.25 to 1.75
- soft_query: bfloat16 [8192, 8192], P('ctx', 'head'), may hold values from -4.5 to 4.5
- soft_key: bfloat16 [8192, 1024], P('ctx', 'head'), may hold values from -4.5 to 4.5
- soft_value: bfloat16 [8192, 1024], P('ctx', 'head'), may hold values from -6 to 6
- doc_lengths: int32 [8], replicated, may hold values from 1 to 4096, 8192 in all
Outputs:
- lin_out: bfloat16 [8192, 8192], P('ctx', 'head')
- soft_out: bfloat16 [8192, 8192], P('ctx', 'head')
The draws below stay inside these ranges and needn't reach their ends.
Inputs may be any that keep to these rules, and one draw needn't show every extreme that they name: `doc_lengths`: the lengths sum to 8192.
All inputs are finite; a program needn't handle non-finite values.
Results may differ from the reference program's by a relative error of at most 0.012.
Values may be sent and summed in bfloat16 or wider, within the bound.
No kernel may reach another device: no remote copies, remote signals or barrier semaphores. Data moves between devices by JAX's collectives and lax.ppermute only.
A program may use at most 128 MiB of HBM per device.

```python
import math
import jax
import jax.numpy as jnp
import numpy as np
from jax import lax

HEADS = 64
KV_HEADS = 8
HEAD_DIM = 128
BLOCK = 256
DOCS = 8
LENGTH = 8192


def draw_soft_query(key, part):
    key = jax.random.fold_in(key, 11)
    base = jnp.clip(jax.random.normal(key, (LENGTH, HEADS * HEAD_DIM), jnp.float32), -4.5, 4.5)
    return base.astype(jnp.bfloat16)


def draw_soft_key(key, part):
    key = jax.random.fold_in(key, 12)
    base = jnp.clip(jax.random.normal(key, (LENGTH, KV_HEADS * HEAD_DIM), jnp.float32), -4.5, 4.5)
    return base.astype(jnp.bfloat16)


def draw_lin_value(key, part):
    key = jax.random.fold_in(key, 5)
    head_of = jnp.arange(HEADS * HEAD_DIM) // HEAD_DIM
    ramp = head_of.astype(jnp.float32) / max(HEADS - 1, 1)
    base = jnp.clip(jax.random.normal(key, (LENGTH, HEADS * HEAD_DIM), jnp.float32), -6.0, 6.0)
    base = base * jnp.power(3.0, ramp)[None, :]
    return base.astype(jnp.bfloat16)


def block_scale(stream_key, dims, shards, smallest, largest):
    gain, own = 1.0, jax.random.fold_in(stream_key, 6)
    for position, parts in shards:
        steps = jnp.exp(jax.random.uniform(jax.random.fold_in(own, position), (parts,), jnp.float32, smallest / len(shards), largest / len(shards)))
        gain = gain * jnp.repeat(steps, dims[position] // parts).reshape([-1 if axis == position else 1 for axis in range(len(dims))])
    return gain


def profile(number_of, total, limit, skew):
    portions = [(1 << 20) // math.isqrt(standing ** skew) + 1 for standing in range(2, number_of + 1)]
    rest, holding = total - limit - (number_of - 1), [1] * (number_of - 1)
    while rest > 0:
        free = [i for i in range(number_of - 1) if holding[i] < limit]
        pool, remaining = sum([portions[i] for i in free]), rest
        for i in free:
            extra = min(limit - holding[i], max(1, remaining * portions[i] // pool), rest)
            holding[i] = holding[i] + extra
            rest = rest - extra
    return np.array([limit] + holding)


def uneven(own_key, count, total, reach, slope):
    if count == 2:
        one = jax.random.randint(own_key, (), max(1, total - reach), min(reach, total - 1) + 1)
        return jnp.stack([one, total - one])
    sizes = jnp.asarray(profile(count, total, reach, slope), jnp.int32)
    twos = (count - 1) // 2
    source_of, taker = sizes[1:1 + 2 * twos:2], sizes[2:2 + 2 * twos:2]
    slack = jnp.minimum(source_of - 1, reach - taker)
    shifted = jax.random.randint(jax.random.fold_in(own_key, 1), (twos,), 0, 1 << 20) % (slack + 1)
    sizes = sizes.at[1:1 + 2 * twos:2].set(source_of - shifted).at[2:2 + 2 * twos:2].set(taker + shifted)
    return sizes[jax.random.permutation(jax.random.fold_in(own_key, 2), count)]


def scatter_about(own_key, dims, spread, most, cuts=(), kind=jnp.bfloat16):
    values = spread * jax.random.normal(own_key, dims, jnp.float32)
    if cuts:
        values = values * block_scale(own_key, dims, cuts, -0.22, 0.18)
    return jnp.clip(values, -most, most).astype(kind)


def setup_inputs(seed: int = 0) -> dict:
    key_list = jax.random.split(jax.random.key(seed), 10)
    return {
        "lin_query": scatter_about(key_list[0], (LENGTH, HEADS * HEAD_DIM), 1.0, 6.0, ((0, 16), (1, 8))),
        "lin_key": scatter_about(key_list[1], (LENGTH, HEADS * HEAD_DIM), 1.0, 6.0, ((0, 16), (1, 8))),
        "lin_value": draw_lin_value(jax.random.fold_in(key_list[9], 71), 0),
        "lin_gate": scatter_about(key_list[3], (LENGTH, HEADS * HEAD_DIM), 1.5, 6.0, ((0, 16), (1, 8))),
        "norm_gain": jnp.clip(1.0 + 0.15 * jax.random.normal(key_list[4], (HEADS * HEAD_DIM,), jnp.float32), 0.25, 1.75),
        "soft_query": draw_soft_query(jax.random.fold_in(key_list[9], 71), 0),
        "soft_key": draw_soft_key(jax.random.fold_in(key_list[9], 71), 0),
        "soft_value": scatter_about(key_list[7], (LENGTH, KV_HEADS * HEAD_DIM), 1.0, 6.0, ((0, 16), (1, 8))),
        "doc_lengths": uneven(key_list[8], DOCS, LENGTH, LENGTH // 2, 2).astype(jnp.int32),
    }


EPS = 1e-06

def doc_index(positions, doc_lengths):
    doc_ends = jnp.cumsum(doc_lengths)
    return lax.optimization_barrier(jnp.sum((doc_ends[None, :] <= positions[:, None]).astype(jnp.int32), axis=1))

def linear_part(lin_query, lin_key, lin_value, doc_lengths):
    blocks = LENGTH // BLOCK
    block_shape = (blocks, BLOCK, HEADS, HEAD_DIM)
    queries = lin_query.reshape(block_shape)
    all_keys = lin_key.reshape(block_shape)
    values = lin_value.reshape(block_shape)
    segments = doc_index(jnp.arange(LENGTH, dtype=jnp.int32), doc_lengths).reshape(blocks, BLOCK)
    previous = doc_index(jnp.arange(blocks, dtype=jnp.int32) * BLOCK - 1, doc_lengths)
    causal = jnp.arange(BLOCK)[:, None] >= jnp.arange(BLOCK)[None, :]

    def block_step(kv_state, inputs):
        query_rows, key_rows, value_rows, segment, prior_doc = inputs
        query_float = query_rows.astype(jnp.float32)
        key_float = key_rows.astype(jnp.float32)
        value_float = value_rows.astype(jnp.float32)
        scores = jnp.einsum('thd,shd->hts', query_float, key_float)
        allowed = causal & (segment[:, None] == segment[None, :])
        weights = jnp.where(allowed[None], scores, 0.0).astype(jnp.bfloat16)
        weights = lax.optimization_barrier(weights).astype(jnp.float32)
        intra_term = jnp.einsum('hts,shd->thd', weights, value_float)
        state_rounded = lax.optimization_barrier(kv_state.astype(jnp.bfloat16)).astype(jnp.float32)
        carried = jnp.einsum('thd,hde->the', query_float, state_rounded)
        inter_term = jnp.where((segment == prior_doc)[:, None, None], carried, 0.0)
        last_doc = segment[-1]
        chosen = (segment == last_doc).astype(jnp.float32)
        update = jnp.einsum('shd,she->hde', key_float * chosen[:, None, None], value_float)
        carry_on = (last_doc == prior_doc).astype(jnp.float32)
        return (carry_on * kv_state + update, intra_term + inter_term)
    initial = jnp.zeros((HEADS, HEAD_DIM, HEAD_DIM), jnp.float32)
    _, linear_raw = lax.scan(block_step, initial, (queries, all_keys, values, segments, previous))
    return linear_raw.reshape(LENGTH, HEADS * HEAD_DIM)

def softmax_part(soft_query, soft_key, soft_value, doc_lengths):
    group_size = HEADS // KV_HEADS
    row_block = math.gcd(LENGTH, 512)
    scale_factor = HEAD_DIM ** (-0.5)
    segments = doc_index(jnp.arange(LENGTH, dtype=jnp.int32), doc_lengths)
    queries = soft_query.reshape(LENGTH, KV_HEADS, group_size, HEAD_DIM).transpose(1, 0, 2, 3)
    all_keys = soft_key.reshape(LENGTH, KV_HEADS, HEAD_DIM).transpose(1, 0, 2)
    values = soft_value.reshape(LENGTH, KV_HEADS, HEAD_DIM).transpose(1, 0, 2)
    outputs = []
    for block_index in range(LENGTH // row_block):
        lower_row = block_index * row_block
        upper_row = lower_row + row_block
        query_pos = jnp.arange(lower_row, upper_row, dtype=jnp.int32)
        key_pos = jnp.arange(upper_row, dtype=jnp.int32)
        allowed = (query_pos[:, None] >= key_pos[None, :]) & (segments[lower_row:upper_row][:, None] == segments[:upper_row][None, :])

        def head_attend(inputs):
            query_rows, key_rows, value_rows = inputs
            scores = jnp.einsum('tgd,sd->tgs', query_rows.astype(jnp.float32), key_rows.astype(jnp.float32)) * scale_factor
            masked = jnp.where(allowed[:, None, :], scores, -jnp.inf)
            row_peak = lax.optimization_barrier(jnp.max(masked, axis=2, keepdims=True))
            weights = jnp.where(allowed[:, None, :], jnp.exp(masked - row_peak), 0.0)
            rounded = lax.optimization_barrier(weights.astype(jnp.bfloat16)).astype(jnp.float32)
            numerator = jnp.einsum('tgs,sd->tgd', rounded, value_rows.astype(jnp.float32))
            return numerator / lax.optimization_barrier(jnp.sum(weights, axis=2, keepdims=True))
        result = lax.map(head_attend, (queries[:, lower_row:upper_row], all_keys[:, :upper_row], values[:, :upper_row]))
        outputs.append(result.transpose(1, 0, 2, 3).reshape(row_block, HEADS * HEAD_DIM))
    return jnp.concatenate(outputs, axis=0).astype(jnp.bfloat16)

def reference(lin_query, lin_key, lin_value, lin_gate, norm_gain, soft_query, soft_key, soft_value, doc_lengths):
    linear_raw = linear_part(lin_query, lin_key, lin_value, doc_lengths)
    mean_square = lax.optimization_barrier(jnp.mean(linear_raw * linear_raw, axis=1))
    inverse_rms = lax.rsqrt(mean_square + EPS)
    gate_values = jax.nn.sigmoid(lin_gate.astype(jnp.float32))
    lin_out = (linear_raw * inverse_rms[:, None] * norm_gain[None, :] * gate_values).astype(jnp.bfloat16)
    soft_out = softmax_part(soft_query, soft_key, soft_value, doc_lengths)
    return (lin_out, soft_out)
```

```python
import functools

import jax
import jax.numpy as jnp
from jax import lax
from jax.experimental import pallas as pl
from jax.experimental.pallas import tpu as pltpu
from jax.sharding import PartitionSpec as P

HEADS = 64
HEAD_DIM = 128
DOCS = 8
EPS = 1e-06
ROWS = 512
LOCAL = 8
WINDOW = 8
FAR = -1.0e4
SCALE = HEAD_DIM**-0.5 * 1.4426950408889634
f32, bf16, i32 = jnp.float32, jnp.bfloat16, jnp.int32

SMEM = pl.BlockSpec(memory_space=pltpu.SMEM)
VMEM = pl.BlockSpec(memory_space=pltpu.VMEM)
ANY = pl.BlockSpec(memory_space=pl.ANY)


def doc_starts(lens):
    starts = [jnp.int32(0)]
    for d in range(DOCS - 1):
        starts.append(starts[-1] + lens[d])
    return starts


def start_of(starts, pos):
    at = starts[0]
    for s in starts[1:]:
        at = jnp.where(pos >= s, s, at)
    return at


def end_of(starts, pos):
    at = jnp.int32(2**30)
    for s in reversed(starts[1:]):
        at = jnp.where(pos < s, s, at)
    return at


def first_row():
    return lax.axis_index("ctx") * ROWS


def dot_nt(a, b):
    return lax.dot_general(a, b, (((1,), (1,)), ((), ())), preferred_element_type=f32)


def dot_tn(a, b):
    return lax.dot_general(a, b, (((0,), (0,)), ((), ())), preferred_element_type=f32)


def head_cols(h):
    return slice(h * HEAD_DIM, (h + 1) * HEAD_DIM)


def state_kernel(place, lens, k_ref, v_ref, u_ref):
    row0 = place[0] * ROWS
    begin = start_of(doc_starts(lens), row0 + ROWS - 1) - row0
    keep = lax.broadcasted_iota(i32, (ROWS, HEAD_DIM), 0) >= begin
    for h in range(k_ref.shape[1] // HEAD_DIM):
        keys = jnp.where(keep, k_ref[:, head_cols(h)].astype(f32), 0.0).astype(bf16)
        u_ref[head_cols(h), :] = dot_tn(keys, v_ref[:, head_cols(h)]).astype(bf16)


def state_call(place, lens, k, v):
    step = 2 * HEAD_DIM
    return pl.pallas_call(
        state_kernel,
        grid=(LOCAL // 2,),
        in_specs=[SMEM, SMEM] + [pl.BlockSpec((ROWS, step), lambda g: (0, g))] * 2,
        out_specs=pl.BlockSpec((step, HEAD_DIM), lambda g: (g, 0)),
        out_shape=jax.ShapeDtypeStruct((LOCAL * HEAD_DIM, HEAD_DIM), bf16),
        cost_estimate=pl.CostEstimate(flops=2 * 10**8, bytes_accessed=2**21, transcendentals=0),
        name="state",
    )(place, lens, k, v)


def join_kernel(distance, place, lens, own_ref, got_ref, out_ref):
    row0 = place[0] * ROWS
    same = start_of(doc_starts(lens), row0 + ROWS - 1) < row0 - (distance - 1) * ROWS
    take = jnp.where(same & (place[0] >= distance), 1.0, 0.0)
    out_ref[...] = (own_ref[...].astype(f32) + take * got_ref[...].astype(f32)).astype(bf16)


def join_call(distance, place, lens, own, got):
    return pl.pallas_call(
        functools.partial(join_kernel, distance),
        in_specs=[SMEM, SMEM, VMEM, VMEM],
        out_specs=VMEM,
        out_shape=jax.ShapeDtypeStruct(own.shape, bf16),
        cost_estimate=pl.CostEstimate(flops=10**6, bytes_accessed=3 * 2**18, transcendentals=0),
        name=f"join{distance}",
    )(place, lens, own, got)


def intra_kernel(place, lens, q_ref, k_ref, v_ref, raw_ref, mask):
    row0 = place[0] * ROWS

    @pl.when(pl.program_id(0) == 0)
    def _():
        starts = doc_starts(lens)
        rows = lax.broadcasted_iota(i32, (ROWS, ROWS), 0)
        cols = lax.broadcasted_iota(i32, (ROWS, ROWS), 1)
        pos = row0 + lax.broadcasted_iota(i32, (ROWS, 1), 0)
        begin = start_of(starts, pos) - row0
        mask[...] = jnp.where((cols <= rows) & (cols >= begin), 1.0, 0.0)

    half = ROWS // 2
    for h in range(q_ref.shape[1] // HEAD_DIM):
        c = head_cols(h)
        for r, width in ((0, half), (half, ROWS)):
            rows = slice(r, r + half)
            s = dot_nt(q_ref[rows, c], k_ref[:width, c]) * mask[rows, :width]
            raw_ref[rows, c] = jnp.dot(s.astype(bf16), v_ref[:width, c], preferred_element_type=f32)


def intra_call(place, lens, q, k, v):
    step = 4 * HEAD_DIM
    block = pl.BlockSpec((ROWS, step), lambda g: (0, g))
    return pl.pallas_call(
        intra_kernel,
        grid=(LOCAL * HEAD_DIM // step,),
        in_specs=[SMEM, SMEM, block, block, block],
        out_specs=block,
        out_shape=jax.ShapeDtypeStruct((ROWS, LOCAL * HEAD_DIM), f32),
        scratch_shapes=[pltpu.VMEM((ROWS, ROWS), f32)],
        cost_estimate=pl.CostEstimate(flops=2 * 10**9, bytes_accessed=5 * 2**20, transcendentals=0),
        name="intra",
    )(place, lens, q, k, v)


def inter_kernel(place, lens, q_ref, near_ref, far_ref, raw_ref, out_ref, square_ref):
    row0 = place[0] * ROWS
    starts = doc_starts(lens)
    reach = jnp.where(place[0] > 0, end_of(starts, row0 - 1) - row0, 0)
    inside = lax.broadcasted_iota(i32, (ROWS, HEAD_DIM), 0) < reach
    take = jnp.where(
        (start_of(starts, row0 - 1) < row0 - 2 * ROWS) & (place[0] >= 3), 1.0, 0.0
    )
    squares = jnp.zeros((ROWS, HEAD_DIM), f32)
    for h in range(LOCAL):
        c = head_cols(h)
        state = (near_ref[c, :].astype(f32) + take * far_ref[c, :].astype(f32)).astype(bf16)
        carried = jnp.dot(q_ref[:, c], state, preferred_element_type=f32)
        raw = raw_ref[:, c] + jnp.where(inside, carried, 0.0)
        out_ref[:, c] = raw
        squares = squares + raw * raw
    ones = jnp.ones((8, HEAD_DIM), f32)
    square_ref[...] = lax.dot_general(
        ones, squares, (((1,), (1,)), ((), ())), precision=lax.Precision.HIGHEST,
        preferred_element_type=f32,
    )


def inter_call(place, lens, q, near, far, raw):
    return pl.pallas_call(
        inter_kernel,
        in_specs=[SMEM, SMEM] + [VMEM] * 4,
        out_specs=(VMEM, VMEM),
        out_shape=(
            jax.ShapeDtypeStruct(raw.shape, f32),
            jax.ShapeDtypeStruct((8, ROWS), f32),
        ),
        input_output_aliases={5: 0},
        cost_estimate=pl.CostEstimate(flops=3 * 10**8, bytes_accessed=5 * 2**20, transcendentals=0),
        name="inter",
    )(place, lens, q, near, far, raw)


def norm_kernel(raw_ref, gate_ref, gain_ref, square_ref, out_ref):
    ones = jnp.full((8, HEAD_DIM), 0.125, f32)
    total = lax.dot_general(
        square_ref[...], ones, (((0,), (0,)), ((), ())), precision=lax.Precision.HIGHEST,
        preferred_element_type=f32,
    )
    inverse = lax.rsqrt(total / (HEADS * HEAD_DIM) + EPS)
    for h in range(raw_ref.shape[1] // HEAD_DIM):
        c = head_cols(h)
        gate = jax.nn.sigmoid(gate_ref[:, c].astype(f32))
        out_ref[:, c] = (raw_ref[:, c] * inverse * gain_ref[:, c] * gate).astype(bf16)


def norm_call(raw, gate, gain, square):
    step = 2 * HEAD_DIM
    block = pl.BlockSpec((ROWS, step), lambda g: (0, g))
    return pl.pallas_call(
        norm_kernel,
        grid=(LOCAL * HEAD_DIM // step,),
        in_specs=[
            block,
            block,
            pl.BlockSpec((1, step), lambda g: (0, g)),
            pl.BlockSpec((8, ROWS), lambda g: (0, 0)),
        ],
        out_specs=block,
        out_shape=jax.ShapeDtypeStruct((ROWS, LOCAL * HEAD_DIM), bf16),
        cost_estimate=pl.CostEstimate(flops=10**7, bytes_accessed=2**22, transcendentals=2**20),
        name="norm",
    )(raw, gate, gain, square)


def attend_kernel(offsets, own, first, last, *refs):
    refs = list(refs)
    place, lens, q_ref = refs[:3]
    del refs[:3]
    count = len(offsets)
    every = tuple(range(WINDOW + 1)) if last else ()
    own_ref = refs.pop(0) if own else None
    shard_refs = [refs.pop(0) for _ in offsets]
    every_refs = [refs.pop(0) for _ in every]
    if not first:
        acc_in, sum_in = refs.pop(0), refs.pop(0)
    if last:
        out_ref = refs.pop(0)
        queries, bias, part, held, sems, acc = refs
    else:
        acc, sum_out = refs.pop(0), refs.pop(0)
        queries, bias, part, held, sems = refs

    row0 = place[0] * ROWS
    starts = doc_starts(lens)
    first_start = start_of(starts, row0)

    def needed(offset):
        begin = row0 - offset * ROWS
        return (begin >= 0) & (first_start < begin + ROWS)

    def copy(ref, slot):
        return pltpu.make_async_copy(ref, held.at[slot], sems.at[slot])

    for slot, offset in enumerate(offsets):

        @pl.when(needed(offset))
        def _(slot=slot):
            copy(shard_refs[slot], slot).start()

    queries[...] = (q_ref[...].astype(f32) * SCALE).astype(bf16)
    part[...] = jnp.zeros_like(part)
    if first:
        acc[...] = jnp.zeros_like(acc)
    else:
        acc[...] = acc_in[...]

    def set_bias(offset, causal):
        pos = row0 + lax.broadcasted_iota(i32, (ROWS, 1), 0)
        begin = start_of(starts, pos)
        keys = row0 - offset * ROWS + lax.broadcasted_iota(i32, (ROWS, ROWS), 1)
        allowed = keys >= begin
        if causal:
            allowed = allowed & (keys <= row0 + lax.broadcasted_iota(i32, (ROWS, ROWS), 0))
        bias[...] = jnp.where(allowed, 0.0, FAR)

    def add(rows, c, keys, values, width):
        s = dot_nt(queries[rows, c], keys) + bias[rows, :width]
        p = jnp.exp2(s)
        acc[rows, c] += jnp.dot(p.astype(bf16), values, preferred_element_type=f32)
        sums = p[:, :HEAD_DIM]
        for at in range(HEAD_DIM, width, HEAD_DIM):
            sums = sums + p[:, at : at + HEAD_DIM]
        part[rows, c] += sums

    if own:
        set_bias(0, True)
        half = ROWS // 2
        for h in range(LOCAL):
            for r, width in ((0, half), (half, ROWS)):
                add(slice(r, r + half), head_cols(h), own_ref[:width, :], own_ref[ROWS : ROWS + width, :], width)

    if count:
        def one(slot, _):
            offset = jnp.int32(offsets[0])
            for i in range(1, count):
                offset = jnp.where(slot == i, offsets[i], offset)

            @pl.when(needed(offset))
            def _():
                copy(shard_refs[0], slot).wait()
                set_bias(offset, False)
                for h in range(LOCAL):
                    add(slice(None), head_cols(h), held[slot, :ROWS, :], held[slot, ROWS:, :], ROWS)

            return 0

        lax.fori_loop(0, count, one, 0)

    lane = lax.broadcasted_iota(i32, (ROWS, HEAD_DIM), 1)
    total = jnp.ones((ROWS, HEAD_DIM), f32)
    if first:
        total = jnp.where(lane < LOCAL, 0.0, total)
    else:
        total = sum_in[...]
    for h in range(LOCAL):
        row_sum = jnp.sum(part[:, head_cols(h)], axis=1, keepdims=True)
        total = jnp.where(lane == h, total + row_sum, total)
    if not last:
        sum_out[...] = total
        return

    for h in range(LOCAL):
        c = head_cols(h)
        out_ref[:, c] = (acc[:, c] / total[:, h : h + 1]).astype(bf16)

    low, high = jnp.min(total), jnp.max(total)

    @pl.when((low < 2.0**-60) | (high > 2.0**100))
    def _():
        acc[...] = jnp.zeros_like(acc)
        part[...] = jnp.where(lax.broadcasted_iota(i32, part.shape, 1) % HEAD_DIM == 0, -1.0e30, 0.0)
        for offset in every:

            @pl.when(needed(offset))
            def _(offset=offset):
                again = pltpu.make_async_copy(every_refs[offset], held.at[0], sems.at[0])
                again.start()
                again.wait()
                set_bias(offset, offset == 0)

                def one_head(h, _):
                    c = pl.ds(pl.multiple_of(h * HEAD_DIM, HEAD_DIM), HEAD_DIM)
                    s = dot_nt(queries[:, c], held[0, :ROWS, :]) + bias[...]
                    old = part[:, c]
                    peak, gone = old[:, 0:1], old[:, 1:2]
                    new = jnp.maximum(peak, jnp.max(s, axis=1, keepdims=True))
                    p = jnp.exp2(s - new)
                    shrink = jnp.exp2(peak - new)
                    acc[:, c] = acc[:, c] * shrink + jnp.dot(
                        p.astype(bf16), held[0, ROWS:, :], preferred_element_type=f32
                    )
                    gone = gone * shrink + jnp.sum(p, axis=1, keepdims=True)
                    part[:, c] = jnp.where(lane == 0, new, gone)
                    return 0

                lax.fori_loop(0, LOCAL, one_head, 0)

        for h in range(LOCAL):
            c = head_cols(h)
            out_ref[:, c] = (acc[:, c] / part[:, c][:, 1:2]).astype(bf16)


def attend_call(place, lens, q, shards, sums, own, offsets, last, name):
    first = sums is None
    wide = q.shape
    operands, specs = [place, lens, q], [SMEM, SMEM, VMEM]
    if own:
        operands.append(shards[0])
        specs.append(VMEM)
    operands += [shards[o] for o in offsets]
    specs += [ANY] * len(offsets)
    if last:
        operands += [shards[o] for o in range(WINDOW + 1)]
        specs += [ANY] * (WINDOW + 1)
    if not first:
        operands += list(sums)
        specs += [VMEM, VMEM]
    scratch = [
        pltpu.VMEM(wide, bf16),
        pltpu.VMEM((ROWS, ROWS), f32),
        pltpu.VMEM(wide, f32),
        pltpu.VMEM((max(1, len(offsets)), 2 * ROWS, HEAD_DIM), bf16),
        pltpu.SemaphoreType.DMA((max(1, len(offsets)),)),
    ]
    if last:
        out_shape = jax.ShapeDtypeStruct(wide, bf16)
        out_specs = VMEM
        scratch.append(pltpu.VMEM(wide, f32))
    else:
        out_shape = (jax.ShapeDtypeStruct(wide, f32), jax.ShapeDtypeStruct((ROWS, HEAD_DIM), f32))
        out_specs = (VMEM, VMEM)
    work = len(offsets) + own
    return pl.pallas_call(
        functools.partial(attend_kernel, tuple(offsets), own, first, last),
        in_specs=specs,
        out_specs=out_specs,
        out_shape=out_shape,
        scratch_shapes=scratch,
        compiler_params=pltpu.CompilerParams(vmem_limit_bytes=32 * 2**20),
        cost_estimate=pl.CostEstimate(
            flops=work * 22 * 10**8, bytes_accessed=4 * 2**20, transcendentals=work * 2**21
        ),
        name=name,
    )(*operands)


def shift(a, distance):
    return lax.ppermute(a, "ctx", [(c, c + distance) for c in range(16 - distance)])


def turn(a, distance):
    return lax.ppermute(
        a, "ctx", [(4 * x + y, 4 * x + (y + distance) % 4) for x in range(4) for y in range(4)]
    )


def head_swap(a, bit):
    return lax.ppermute(a, "head", [(i, i ^ bit) for i in range(8)])


def body(
    lin_query, lin_key, lin_value, lin_gate, norm_gain, soft_query, soft_key, soft_value, doc_lengths
):
    ctx = lax.axis_index("ctx")
    place = jnp.reshape(ctx, (1,))
    y = ctx % 4
    gain = norm_gain.reshape(1, -1)

    own = jnp.concatenate([soft_key, soft_value], axis=0)
    shards = {0: own}
    shards[4] = shift(own, 4)
    shards[8] = shift(own, 8)

    state = state_call(place, doc_lengths, lin_key, lin_value)
    pair = join_call(4, place, doc_lengths, state, shift(state, 4))
    four = join_call(1, place, doc_lengths, pair, shift(pair, 1))
    near, far = shift(four, 1), shift(four, 3)

    seam_up, seam_down = y == 3, y == 0
    shards[1] = turn(jnp.where(seam_up, shards[4], own), 1)
    shards[3] = turn(jnp.where(seam_down, own, shards[4]), 3)
    shards[5] = turn(jnp.where(seam_up, shards[8], shards[4]), 1)
    shards[7] = turn(jnp.where(seam_down, shards[4], shards[8]), 3)
    shards[2] = turn(jnp.where(seam_up, shards[5], shards[1]), 1)
    shards[6] = turn(jnp.where(seam_down, shards[3], shards[7]), 3)

    raw = intra_call(place, doc_lengths, lin_query, lin_key, lin_value)
    sums = attend_call(place, doc_lengths, soft_query, shards, None, True, (4, 8), False, "attend_a")
    sums = attend_call(place, doc_lengths, soft_query, shards, sums, False, (1, 3, 5, 7), False, "attend_b")

    raw, square = inter_call(place, doc_lengths, lin_query, near, far, raw)
    for bit in (1, 2, 4):
        square = square + head_swap(square, bit)
    lin_out = norm_call(raw, lin_gate, gain, square)

    soft_out = attend_call(place, doc_lengths, soft_query, shards, sums, False, (2, 6), True, "attend_c")
    return lin_out, soft_out


def solution(mesh):
    split = P("ctx", "head")
    return jax.shard_map(
        body,
        mesh=mesh,
        in_specs=(split, split, split, split, P("head"), split, split, split, P()),
        out_specs=(split, split),
        check_vma=False,
    )
```

```python
import functools

import jax
import jax.numpy as jnp
from jax import lax
from jax.experimental import pallas as pl
from jax.experimental.pallas import tpu as pltpu
from jax.sharding import PartitionSpec as P

HEADS = 64
HEAD_DIM = 128
DOCS = 8
EPS = 1e-06
ROWS = 512
LOCAL = 8
WINDOW = 8
FAR = -1.0e4
SCALE = HEAD_DIM**-0.5 * 1.4426950408889634
f32, bf16, i32 = jnp.float32, jnp.bfloat16, jnp.int32

SMEM = pl.BlockSpec(memory_space=pltpu.SMEM)
VMEM = pl.BlockSpec(memory_space=pltpu.VMEM)
ANY = pl.BlockSpec(memory_space=pl.ANY)
LIGHT = pl.CostEstimate(flops=10**6, bytes_accessed=2**16, transcendentals=0)
SMALL = pltpu.CompilerParams(vmem_limit_bytes=16 * 2**20)


def doc_starts(lens):
    starts = [jnp.int32(0)]
    for d in range(DOCS - 1):
        starts.append(starts[-1] + lens[d])
    return starts


def start_of(starts, pos):
    at = starts[0]
    for s in starts[1:]:
        at = jnp.where(pos >= s, s, at)
    return at


def end_of(starts, pos):
    at = jnp.int32(2**30)
    for s in reversed(starts[1:]):
        at = jnp.where(pos < s, s, at)
    return at


def first_row():
    return lax.axis_index("ctx") * ROWS


def dot_nt(a, b):
    return lax.dot_general(a, b, (((1,), (1,)), ((), ())), preferred_element_type=f32)


def dot_tn(a, b):
    return lax.dot_general(a, b, (((0,), (0,)), ((), ())), preferred_element_type=f32)


def head_cols(h):
    return slice(h * HEAD_DIM, (h + 1) * HEAD_DIM)


def linear_kernel(place, lens, q_ref, k_ref, v_ref, raw_ref, state_ref, mask):
    row0 = place[0] * ROWS
    starts = doc_starts(lens)

    @pl.when(pl.program_id(0) == 0)
    def _():
        rows = lax.broadcasted_iota(i32, (ROWS, ROWS), 0)
        cols = lax.broadcasted_iota(i32, (ROWS, ROWS), 1)
        pos = row0 + lax.broadcasted_iota(i32, (ROWS, 1), 0)
        begin = start_of(starts, pos) - row0
        mask[...] = jnp.where((cols <= rows) & (cols >= begin), 1.0, 0.0).astype(bf16)

    last_begin = start_of(starts, row0 + ROWS - 1) - row0
    keep = lax.broadcasted_iota(i32, (HEAD_DIM, ROWS), 1) >= last_begin
    keep = jnp.where(keep, 1.0, 0.0).astype(bf16)
    half = ROWS // 2
    for h in range(q_ref.shape[1] // HEAD_DIM):
        c = head_cols(h)
        state_ref[c, :] = jnp.dot(
            k_ref[:, c].T * keep, v_ref[:, c], preferred_element_type=f32
        ).astype(bf16)
        for r, width in ((0, half), (half, ROWS)):
            rows = slice(r, r + half)
            s = dot_nt(q_ref[rows, c], k_ref[:width, c]).astype(bf16) * mask[rows, :width]
            raw_ref[rows, c] = jnp.dot(s, v_ref[:width, c], preferred_element_type=f32)


def linear_call(place, lens, q, k, v):
    step = 4 * HEAD_DIM
    block = pl.BlockSpec((ROWS, step), lambda g: (0, g))
    return pl.pallas_call(
        linear_kernel,
        grid=(LOCAL * HEAD_DIM // step,),
        in_specs=[SMEM, SMEM, block, block, block],
        out_specs=(block, pl.BlockSpec((step, HEAD_DIM), lambda g: (g, 0))),
        out_shape=(
            jax.ShapeDtypeStruct((ROWS, LOCAL * HEAD_DIM), f32),
            jax.ShapeDtypeStruct((LOCAL * HEAD_DIM, HEAD_DIM), bf16),
        ),
        scratch_shapes=[pltpu.VMEM((ROWS, ROWS), bf16)],
        cost_estimate=LIGHT,
        name="linear",
    )(place, lens, q, k, v)


def join_kernel(distance, place, lens, own_ref, got_ref, out_ref):
    row0 = place[0] * ROWS
    same = start_of(doc_starts(lens), row0 + ROWS - 1) < row0 - (distance - 1) * ROWS
    take = jnp.where(same & (place[0] >= distance), 1.0, 0.0)
    out_ref[...] = (own_ref[...].astype(f32) + take * got_ref[...].astype(f32)).astype(bf16)


def join_call(distance, place, lens, own, got):
    return pl.pallas_call(
        functools.partial(join_kernel, distance),
        in_specs=[SMEM, SMEM, VMEM, VMEM],
        out_specs=VMEM,
        out_shape=jax.ShapeDtypeStruct(own.shape, bf16),
        compiler_params=SMALL,
        cost_estimate=LIGHT,
        name=f"join{distance}",
    )(place, lens, own, got)


def inter_kernel(place, lens, q_ref, near_ref, far_ref, raw_ref, out_ref, square_ref):
    row0 = place[0] * ROWS
    starts = doc_starts(lens)
    reach = jnp.where(place[0] > 0, end_of(starts, row0 - 1) - row0, 0)
    inside = lax.broadcasted_iota(i32, (ROWS, HEAD_DIM), 0) < reach
    take = jnp.where(
        (start_of(starts, row0 - 1) < row0 - 2 * ROWS) & (place[0] >= 3), 1.0, 0.0
    )
    squares = jnp.zeros((ROWS, HEAD_DIM), f32)
    for h in range(LOCAL):
        c = head_cols(h)
        state = (near_ref[c, :].astype(f32) + take * far_ref[c, :].astype(f32)).astype(bf16)
        carried = jnp.dot(q_ref[:, c], state, preferred_element_type=f32)
        raw = raw_ref[:, c] + jnp.where(inside, carried, 0.0)
        out_ref[:, c] = raw
        squares = squares + raw * raw
    ones = jnp.ones((8, HEAD_DIM), f32)
    square_ref[...] = lax.dot_general(
        ones, squares, (((1,), (1,)), ((), ())), precision=lax.Precision.HIGHEST,
        preferred_element_type=f32,
    )


def inter_call(place, lens, q, near, far, raw):
    return pl.pallas_call(
        inter_kernel,
        in_specs=[SMEM, SMEM] + [VMEM] * 4,
        out_specs=(VMEM, VMEM),
        out_shape=(
            jax.ShapeDtypeStruct(raw.shape, f32),
            jax.ShapeDtypeStruct((8, ROWS), f32),
        ),
        input_output_aliases={5: 0},
        compiler_params=SMALL,
        cost_estimate=LIGHT,
        name="inter",
    )(place, lens, q, near, far, raw)


def norm_kernel(raw_ref, gate_ref, gain_ref, near_ref, far_ref, out_ref, inverse):
    @pl.when(pl.program_id(0) == 0)
    def _():
        ones = jnp.full((8, HEAD_DIM), 0.125, f32)
        total = lax.dot_general(
            near_ref[...] + far_ref[...], ones, (((0,), (0,)), ((), ())),
            precision=lax.Precision.HIGHEST, preferred_element_type=f32,
        )
        inverse[...] = lax.rsqrt(total / (HEADS * HEAD_DIM) + EPS)

    for h in range(raw_ref.shape[1] // HEAD_DIM):
        c = head_cols(h)
        gate = jax.nn.sigmoid(gate_ref[:, c].astype(f32))
        out_ref[:, c] = (raw_ref[:, c] * inverse[...] * gain_ref[:, c] * gate).astype(bf16)


def norm_call(raw, gate, gain, near, far):
    step = 4 * HEAD_DIM
    block = pl.BlockSpec((ROWS, step), lambda g: (0, g))
    square = pl.BlockSpec((8, ROWS), lambda g: (0, 0))
    return pl.pallas_call(
        norm_kernel,
        grid=(LOCAL * HEAD_DIM // step,),
        in_specs=[block, block, pl.BlockSpec((1, step), lambda g: (0, g)), square, square],
        out_specs=block,
        out_shape=jax.ShapeDtypeStruct((ROWS, LOCAL * HEAD_DIM), bf16),
        scratch_shapes=[pltpu.VMEM((ROWS, HEAD_DIM), f32)],
        compiler_params=SMALL,
        cost_estimate=LIGHT,
        name="norm",
    )(raw, gate, gain, near, far)


def attend_kernel(offsets, own, first, last, *refs):
    refs = list(refs)
    place, lens, q_ref = refs[:3]
    del refs[:3]
    count = len(offsets)
    every = tuple(range(WINDOW + 1)) if last else ()
    own_ref = refs.pop(0) if own else None
    shard_refs = [refs.pop(0) for _ in offsets]
    every_refs = [refs.pop(0) for _ in every]
    if not first:
        acc, part = refs.pop(0), refs.pop(0)
    if last:
        out_ref = refs.pop(0)
    else:
        acc, part = refs.pop(0), refs.pop(0)
    if first:
        queries = refs.pop(0)
    else:
        queries = q_ref
    bias, held, sems = refs

    row0 = place[0] * ROWS
    starts = doc_starts(lens)
    first_start, last_start = start_of(starts, row0), start_of(starts, row0 + ROWS - 1)

    def needed(offset):
        begin = row0 - offset * ROWS
        return (begin >= 0) & (first_start < begin + ROWS)

    def copy(ref, slot):
        return pltpu.make_async_copy(ref, held.at[slot], sems.at[slot])

    for slot, offset in enumerate(offsets):

        @pl.when(needed(offset))
        def _(slot=slot):
            copy(shard_refs[slot], slot).start()

    if first:
        queries[...] = (q_ref[...].astype(f32) * SCALE).astype(bf16)
        part[...] = jnp.zeros_like(part)
        acc[...] = jnp.zeros_like(acc)

    def set_bias(offset, causal):
        pos = row0 + lax.broadcasted_iota(i32, (ROWS, 1), 0)
        begin = start_of(starts, pos)
        keys = row0 - offset * ROWS + lax.broadcasted_iota(i32, (ROWS, ROWS), 1)
        allowed = keys >= begin
        if causal:
            allowed = allowed & (keys <= row0 + lax.broadcasted_iota(i32, (ROWS, ROWS), 0))
        bias[...] = jnp.where(allowed, 0.0, FAR)

    def add(rows, c, keys, values, width, masked):
        s = dot_nt(queries[rows, c], keys)
        if masked:
            s = s + bias[rows, :width]
        p = jnp.exp2(s)
        acc[rows, c] += jnp.dot(p.astype(bf16), values, preferred_element_type=f32)
        sums = p[:, :HEAD_DIM]
        for at in range(HEAD_DIM, width, HEAD_DIM):
            sums = sums + p[:, at : at + HEAD_DIM]
        part[rows, c] += sums

    if own:
        set_bias(0, True)
        half = ROWS // 2
        for h in range(LOCAL):
            for r, width in ((0, half), (half, ROWS)):
                rows = slice(r, r + half)
                add(rows, head_cols(h), own_ref[:width, :], own_ref[ROWS : ROWS + width, :], width, True)

    def one(slot, _):
        offset = jnp.int32(offsets[0])
        for i in range(1, count):
            offset = jnp.where(slot == i, offsets[i], offset)
        use = needed(offset)
        free = last_start <= row0 - offset * ROWS

        def every_head(masked):
            for h in range(LOCAL):
                add(slice(None), head_cols(h), held[slot, :ROWS, :], held[slot, ROWS:, :], ROWS, masked)

        @pl.when(use)
        def _():
            copy(shard_refs[0], slot).wait()

        @pl.when(use)
        def _():
            @pl.when(free)
            def _():
                bias[...] = jnp.zeros_like(bias)

            @pl.when(jnp.logical_not(free))
            def _():
                set_bias(offset, False)

            every_head(True)

        return 0

    if count:
        lax.fori_loop(0, count, one, 0)
    if not last:
        return

    low = high = jnp.ones((ROWS, 1), f32)
    for h in range(LOCAL):
        c = head_cols(h)
        total = jnp.sum(part[:, c], axis=1, keepdims=True)
        low, high = jnp.minimum(low, total), jnp.maximum(high, total)
        out_ref[:, c] = (acc[:, c] / total).astype(bf16)

    @pl.when((jnp.min(low) < 2.0**-60) | (jnp.max(high) > 2.0**100))
    def _():
        lane = lax.broadcasted_iota(i32, (ROWS, HEAD_DIM), 1)
        acc[...] = jnp.zeros_like(acc)
        for h in range(LOCAL):
            part[:, head_cols(h)] = jnp.where(lane == 0, -1.0e30, 0.0)
        for offset in every:

            @pl.when(needed(offset))
            def _(offset=offset):
                again = pltpu.make_async_copy(every_refs[offset], held.at[0], sems.at[0])
                again.start()
                again.wait()
                set_bias(offset, offset == 0)

                def one_head(h, _):
                    c = pl.ds(pl.multiple_of(h * HEAD_DIM, HEAD_DIM), HEAD_DIM)
                    s = dot_nt(queries[:, c], held[0, :ROWS, :]) + bias[...]
                    old = part[:, c]
                    peak, gone = old[:, 0:1], old[:, 1:2]
                    new = jnp.maximum(peak, jnp.max(s, axis=1, keepdims=True))
                    p = jnp.exp2(s - new)
                    shrink = jnp.exp2(peak - new)
                    acc[:, c] = acc[:, c] * shrink + jnp.dot(
                        p.astype(bf16), held[0, ROWS:, :], preferred_element_type=f32
                    )
                    gone = gone * shrink + jnp.sum(p, axis=1, keepdims=True)
                    part[:, c] = jnp.where(lane == 0, new, gone)
                    return 0

                lax.fori_loop(0, LOCAL, one_head, 0)

        for h in range(LOCAL):
            c = head_cols(h)
            out_ref[:, c] = (acc[:, c] / part[:, c][:, 1:2]).astype(bf16)


def attend_call(place, lens, q, shards, sums, own, offsets, last, name):
    first = sums is None
    wide = q.shape
    operands, specs = [place, lens, q if first else sums[2]], [SMEM, SMEM, VMEM]
    if own:
        operands.append(shards[0])
        specs.append(VMEM)
    operands += [shards[o] for o in offsets]
    specs += [ANY] * len(offsets)
    if last:
        operands += [shards[o] for o in range(WINDOW + 1)]
        specs += [ANY] * (WINDOW + 1)
    if not first:
        operands += list(sums[:2])
        specs += [VMEM, VMEM]
    scratch = [
        pltpu.VMEM((ROWS, ROWS), f32),
        pltpu.VMEM((max(1, len(offsets)), 2 * ROWS, HEAD_DIM), bf16),
        pltpu.SemaphoreType.DMA((max(1, len(offsets)),)),
    ]
    aliases = {}
    if last:
        out_shape = jax.ShapeDtypeStruct(wide, bf16)
        out_specs = VMEM
    else:
        out_shape = [jax.ShapeDtypeStruct(wide, f32)] * 2
        if first:
            out_shape.append(jax.ShapeDtypeStruct(wide, bf16))
        else:
            aliases = {len(operands) - 2: 0, len(operands) - 1: 1}
        out_specs = [VMEM] * len(out_shape)
    result = pl.pallas_call(
        functools.partial(attend_kernel, tuple(offsets), own, first, last),
        input_output_aliases=aliases,
        in_specs=specs,
        out_specs=out_specs,
        out_shape=out_shape,
        scratch_shapes=scratch,
        compiler_params=pltpu.CompilerParams(vmem_limit_bytes=20 * 2**20),
        cost_estimate=LIGHT,
        name=name,
    )(*operands)
    if last or first:
        return result
    return [*result, sums[2]]


def rotate(a, distance):
    return lax.ppermute(a, "ctx", [(c, (c + distance) % 16) for c in range(16)])


def turn(a, distance):
    return lax.ppermute(
        a, "ctx", [(4 * x + y, 4 * x + (y + distance) % 4) for x in range(4) for y in range(4)]
    )


def head_swap(a, bit):
    return lax.ppermute(a, "head", [(i, i ^ bit) for i in range(8)])


def after(a, *others):
    return lax.optimization_barrier((a, *others))[0]


def body(
    lin_query, lin_key, lin_value, lin_gate, norm_gain, soft_query, soft_key, soft_value, doc_lengths
):
    place = jnp.reshape(lax.axis_index("ctx"), (1,))
    y = lax.axis_index("ctx") % 4
    gain = norm_gain.reshape(1, -1)

    def behind(distance, here, there):
        return turn(jnp.where(y >= 4 - distance, there, here), distance)

    def attend(place, sums, own, offsets, last, name):
        return attend_call(place, doc_lengths, soft_query, shards, sums, own, offsets, last, name)

    own = jnp.concatenate([soft_key, soft_value], axis=0)
    shards = {0: own}
    shards[4] = rotate(own, 4)
    shards[8] = rotate(own, 8)

    raw, state = linear_call(after(place, own), doc_lengths, lin_query, lin_key, lin_value)
    state_before = rotate(state, 4)
    for k in (1, 3, 2):
        shards[k] = behind(k, after(own, state), shards[4])
    sums = attend(after(place, state), None, True, (4,), False, "attend_a")

    pair = join_call(4, after(place, sums[1]), doc_lengths, state, state_before)
    pair_before = rotate(pair, 1)
    for k in (1, 3, 2):
        shards[k + 4] = behind(k, after(shards[4], pair), shards[8])
    sums = attend(after(place, pair), sums, False, (8, 1), False, "attend_b")

    four = join_call(1, after(place, sums[1]), doc_lengths, pair, pair_before)
    near, far = rotate(four, 1), rotate(four, 3)
    sums = attend(after(place, four), sums, False, (3, 2), False, "attend_c")

    raw, square = inter_call(after(place, sums[1]), doc_lengths, lin_query, near, far, raw)
    for bit in (1, 2):
        square = square + head_swap(square, bit)
    soft_out = attend(after(place, square), sums, False, (5, 7, 6), True, "attend_d")
    lin_out = norm_call(raw, lin_gate, gain, square, head_swap(square, 4))
    return lin_out, soft_out


def solution(mesh):
    split = P("ctx", "head")
    return jax.shard_map(
        body,
        mesh=mesh,
        in_specs=(split, split, split, split, P("head"), split, split, split, P()),
        out_specs=(split, split),
        check_vma=False,
    )
```

```python
import functools

import jax
import jax.numpy as jnp
from jax import lax
from jax.experimental import pallas as pl
from jax.experimental.pallas import tpu as pltpu
from jax.sharding import PartitionSpec as P

HEADS = 64
HEAD_DIM = 128
DOCS = 8
EPS = 1e-06
ROWS = 512
LOCAL = 8
WINDOW = 8
FAR = -1.0e4
SCALE = HEAD_DIM**-0.5 * 1.4426950408889634
f32, bf16, i32 = jnp.float32, jnp.bfloat16, jnp.int32

SMEM = pl.BlockSpec(memory_space=pltpu.SMEM)
VMEM = pl.BlockSpec(memory_space=pltpu.VMEM)
ANY = pl.BlockSpec(memory_space=pl.ANY)
LIGHT = pl.CostEstimate(flops=10**6, bytes_accessed=2**16, transcendentals=0)
SMALL = pltpu.CompilerParams(vmem_limit_bytes=16 * 2**20)


def doc_starts(lens):
    starts = [jnp.int32(0)]
    for d in range(DOCS - 1):
        starts.append(starts[-1] + lens[d])
    return starts


def start_of(starts, pos):
    at = starts[0]
    for s in starts[1:]:
        at = jnp.where(pos >= s, s, at)
    return at


def end_of(starts, pos):
    at = jnp.int32(2**30)
    for s in reversed(starts[1:]):
        at = jnp.where(pos < s, s, at)
    return at


def first_row():
    return lax.axis_index("ctx") * ROWS


def dot_nt(a, b):
    return lax.dot_general(a, b, (((1,), (1,)), ((), ())), preferred_element_type=f32)


def dot_tn(a, b):
    return lax.dot_general(a, b, (((0,), (0,)), ((), ())), preferred_element_type=f32)


def head_cols(h):
    return slice(h * HEAD_DIM, (h + 1) * HEAD_DIM)


def linear_kernel(place, lens, q_ref, k_ref, v_ref, raw_ref, state_ref, mask):
    row0 = place[0] * ROWS
    starts = doc_starts(lens)

    @pl.when(pl.program_id(0) == 0)
    def _():
        rows = lax.broadcasted_iota(i32, (ROWS, ROWS), 0)
        cols = lax.broadcasted_iota(i32, (ROWS, ROWS), 1)
        pos = row0 + lax.broadcasted_iota(i32, (ROWS, 1), 0)
        begin = start_of(starts, pos) - row0
        mask[...] = jnp.where((cols <= rows) & (cols >= begin), 1.0, 0.0).astype(bf16)

    last_begin = start_of(starts, row0 + ROWS - 1) - row0
    keep = lax.broadcasted_iota(i32, (HEAD_DIM, ROWS), 1) >= last_begin
    keep = jnp.where(keep, 1.0, 0.0).astype(bf16)
    half = ROWS // 2
    for h in range(q_ref.shape[1] // HEAD_DIM):
        c = head_cols(h)
        state_ref[c, :] = jnp.dot(
            k_ref[:, c].T * keep, v_ref[:, c], preferred_element_type=f32
        ).astype(bf16)
        for r, width in ((0, half), (half, ROWS)):
            rows = slice(r, r + half)
            s = dot_nt(q_ref[rows, c], k_ref[:width, c]).astype(bf16) * mask[rows, :width]
            raw_ref[rows, c] = jnp.dot(s, v_ref[:width, c], preferred_element_type=f32)


def linear_call(place, lens, q, k, v):
    step = 4 * HEAD_DIM
    block = pl.BlockSpec((ROWS, step), lambda g: (0, g))
    return pl.pallas_call(
        linear_kernel,
        grid=(LOCAL * HEAD_DIM // step,),
        in_specs=[SMEM, SMEM, block, block, block],
        out_specs=(block, pl.BlockSpec((step, HEAD_DIM), lambda g: (g, 0))),
        out_shape=(
            jax.ShapeDtypeStruct((ROWS, LOCAL * HEAD_DIM), f32),
            jax.ShapeDtypeStruct((LOCAL * HEAD_DIM, HEAD_DIM), bf16),
        ),
        scratch_shapes=[pltpu.VMEM((ROWS, ROWS), bf16)],
        cost_estimate=LIGHT,
        name="linear",
    )(place, lens, q, k, v)


def join_kernel(distance, place, lens, own_ref, got_ref, out_ref):
    row0 = place[0] * ROWS
    same = start_of(doc_starts(lens), row0 + ROWS - 1) < row0 - (distance - 1) * ROWS
    take = jnp.where(same & (place[0] >= distance), 1.0, 0.0)
    out_ref[...] = (own_ref[...].astype(f32) + take * got_ref[...].astype(f32)).astype(bf16)


def join_call(distance, place, lens, own, got):
    return pl.pallas_call(
        functools.partial(join_kernel, distance),
        in_specs=[SMEM, SMEM, VMEM, VMEM],
        out_specs=VMEM,
        out_shape=jax.ShapeDtypeStruct(own.shape, bf16),
        compiler_params=SMALL,
        cost_estimate=LIGHT,
        name=f"join{distance}",
    )(place, lens, own, got)


def inter_kernel(place, lens, q_ref, near_ref, far_ref, raw_ref, out_ref, square_ref):
    row0 = place[0] * ROWS
    starts = doc_starts(lens)
    reach = jnp.where(place[0] > 0, end_of(starts, row0 - 1) - row0, 0)
    inside = lax.broadcasted_iota(i32, (ROWS, HEAD_DIM), 0) < reach
    take = jnp.where(
        (start_of(starts, row0 - 1) < row0 - 2 * ROWS) & (place[0] >= 3), 1.0, 0.0
    )
    squares = jnp.zeros((ROWS, HEAD_DIM), f32)
    for h in range(LOCAL):
        c = head_cols(h)
        state = (near_ref[c, :].astype(f32) + take * far_ref[c, :].astype(f32)).astype(bf16)
        carried = jnp.dot(q_ref[:, c], state, preferred_element_type=f32)
        raw = raw_ref[:, c] + jnp.where(inside, carried, 0.0)
        out_ref[:, c] = raw
        squares = squares + raw * raw
    ones = jnp.ones((8, HEAD_DIM), f32)
    square_ref[...] = lax.dot_general(
        ones, squares, (((1,), (1,)), ((), ())), precision=lax.Precision.HIGHEST,
        preferred_element_type=f32,
    )


def inter_call(place, lens, q, near, far, raw):
    return pl.pallas_call(
        inter_kernel,
        in_specs=[SMEM, SMEM] + [VMEM] * 4,
        out_specs=(VMEM, VMEM),
        out_shape=(
            jax.ShapeDtypeStruct(raw.shape, f32),
            jax.ShapeDtypeStruct((8, ROWS), f32),
        ),
        input_output_aliases={5: 0},
        compiler_params=SMALL,
        cost_estimate=LIGHT,
        name="inter",
    )(place, lens, q, near, far, raw)


def norm_kernel(raw_ref, gate_ref, gain_ref, near_ref, far_ref, out_ref, inverse):
    @pl.when(pl.program_id(0) == 0)
    def _():
        ones = jnp.full((8, HEAD_DIM), 0.125, f32)
        total = lax.dot_general(
            near_ref[...] + far_ref[...], ones, (((0,), (0,)), ((), ())),
            precision=lax.Precision.HIGHEST, preferred_element_type=f32,
        )
        inverse[...] = lax.rsqrt(total / (HEADS * HEAD_DIM) + EPS)

    for h in range(raw_ref.shape[1] // HEAD_DIM):
        c = head_cols(h)
        gate = jax.nn.sigmoid(gate_ref[:, c].astype(f32))
        out_ref[:, c] = (raw_ref[:, c] * inverse[...] * gain_ref[:, c] * gate).astype(bf16)


def norm_call(raw, gate, gain, near, far):
    step = 4 * HEAD_DIM
    block = pl.BlockSpec((ROWS, step), lambda g: (0, g))
    square = pl.BlockSpec((8, ROWS), lambda g: (0, 0))
    return pl.pallas_call(
        norm_kernel,
        grid=(LOCAL * HEAD_DIM // step,),
        in_specs=[block, block, pl.BlockSpec((1, step), lambda g: (0, g)), square, square],
        out_specs=block,
        out_shape=jax.ShapeDtypeStruct((ROWS, LOCAL * HEAD_DIM), bf16),
        scratch_shapes=[pltpu.VMEM((ROWS, HEAD_DIM), f32)],
        compiler_params=SMALL,
        cost_estimate=LIGHT,
        name="norm",
    )(raw, gate, gain, near, far)


def attend_kernel(offsets, own, first, last, *refs):
    refs = list(refs)
    place, lens, q_ref = refs[:3]
    del refs[:3]
    count = len(offsets)
    every = tuple(range(WINDOW + 1)) if last else ()
    own_ref = refs.pop(0) if own else None
    shard_refs = [refs.pop(0) for _ in offsets]
    every_refs = [refs.pop(0) for _ in every]
    if not first:
        acc, part = refs.pop(0), refs.pop(0)
    if last:
        out_ref = refs.pop(0)
    else:
        acc, part = refs.pop(0), refs.pop(0)
    if first:
        queries = refs.pop(0)
    else:
        queries = q_ref
    bias, held, sems = refs

    row0 = place[0] * ROWS
    starts = doc_starts(lens)
    first_start, last_start = start_of(starts, row0), start_of(starts, row0 + ROWS - 1)

    def needed(offset):
        begin = row0 - offset * ROWS
        return (begin >= 0) & (first_start < begin + ROWS)

    def copy(ref, slot):
        return pltpu.make_async_copy(ref, held.at[slot], sems.at[slot])

    for slot, offset in enumerate(offsets):

        @pl.when(needed(offset))
        def _(slot=slot):
            copy(shard_refs[slot], slot).start()

    if first:
        queries[...] = (q_ref[...].astype(f32) * SCALE).astype(bf16)
        part[...] = jnp.zeros_like(part)
        acc[...] = jnp.zeros_like(acc)

    def set_bias(offset, causal):
        pos = row0 + lax.broadcasted_iota(i32, (ROWS, 1), 0)
        begin = start_of(starts, pos)
        keys = row0 - offset * ROWS + lax.broadcasted_iota(i32, (ROWS, ROWS), 1)
        allowed = keys >= begin
        if causal:
            allowed = allowed & (keys <= row0 + lax.broadcasted_iota(i32, (ROWS, ROWS), 0))
        bias[...] = jnp.where(allowed, 0.0, FAR)

    def add(rows, c, keys, values, width, masked):
        s = dot_nt(queries[rows, c], keys)
        if masked:
            s = s + bias[rows, :width]
        p = jnp.exp2(s)
        acc[rows, c] += jnp.dot(p.astype(bf16), values, preferred_element_type=f32)
        sums = p[:, :HEAD_DIM]
        for at in range(HEAD_DIM, width, HEAD_DIM):
            sums = sums + p[:, at : at + HEAD_DIM]
        part[rows, c] += sums

    if own:
        set_bias(0, True)
        half = ROWS // 2
        for h in range(LOCAL):
            for r, width in ((0, half), (half, ROWS)):
                rows = slice(r, r + half)
                add(rows, head_cols(h), own_ref[:width, :], own_ref[ROWS : ROWS + width, :], width, True)

    def one(slot, _):
        offset = jnp.int32(offsets[0])
        for i in range(1, count):
            offset = jnp.where(slot == i, offsets[i], offset)
        use = needed(offset)
        free = last_start <= row0 - offset * ROWS

        def every_head(masked):
            for h in range(LOCAL):
                add(slice(None), head_cols(h), held[slot, :ROWS, :], held[slot, ROWS:, :], ROWS, masked)

        @pl.when(use)
        def _():
            copy(shard_refs[0], slot).wait()

        @pl.when(use)
        def _():
            @pl.when(free)
            def _():
                bias[...] = jnp.zeros_like(bias)

            @pl.when(jnp.logical_not(free))
            def _():
                set_bias(offset, False)

            every_head(True)

        return 0

    if count:
        lax.fori_loop(0, count, one, 0)
    if not last:
        return

    low = high = jnp.ones((ROWS, 1), f32)
    for h in range(LOCAL):
        c = head_cols(h)
        total = jnp.sum(part[:, c], axis=1, keepdims=True)
        low, high = jnp.minimum(low, total), jnp.maximum(high, total)
        out_ref[:, c] = (acc[:, c] / total).astype(bf16)

    @pl.when((jnp.min(low) < 2.0**-60) | (jnp.max(high) > 2.0**100))
    def _():
        lane = lax.broadcasted_iota(i32, (ROWS, HEAD_DIM), 1)
        acc[...] = jnp.zeros_like(acc)
        for h in range(LOCAL):
            part[:, head_cols(h)] = jnp.where(lane == 0, -1.0e30, 0.0)
        def again(offset, _):
            for k in every:

                @pl.when(offset == k)
                def _(k=k):
                    fetch = pltpu.make_async_copy(every_refs[k], held.at[0], sems.at[0])
                    fetch.start()
                    fetch.wait()

            set_bias(offset, True)

            def one_head(h, _):
                c = pl.ds(pl.multiple_of(h * HEAD_DIM, HEAD_DIM), HEAD_DIM)
                s = dot_nt(queries[:, c], held[0, :ROWS, :]) + bias[...]
                old = part[:, c]
                peak, gone = old[:, 0:1], old[:, 1:2]
                new = jnp.maximum(peak, jnp.max(s, axis=1, keepdims=True))
                p = jnp.exp2(s - new)
                shrink = jnp.exp2(peak - new)
                acc[:, c] = acc[:, c] * shrink + jnp.dot(
                    p.astype(bf16), held[0, ROWS:, :], preferred_element_type=f32
                )
                gone = gone * shrink + jnp.sum(p, axis=1, keepdims=True)
                part[:, c] = jnp.where(lane == 0, new, gone)
                return 0

            lax.fori_loop(0, LOCAL, one_head, 0)
            return 0

        lax.fori_loop(0, jnp.minimum(place[0], WINDOW) + 1, again, 0)
        for h in range(LOCAL):
            c = head_cols(h)
            out_ref[:, c] = (acc[:, c] / part[:, c][:, 1:2]).astype(bf16)


def attend_call(place, lens, q, shards, sums, own, offsets, last, name):
    first = sums is None
    wide = q.shape
    operands, specs = [place, lens, q if first else sums[2]], [SMEM, SMEM, VMEM]
    if own:
        operands.append(shards[0])
        specs.append(VMEM)
    operands += [shards[o] for o in offsets]
    specs += [ANY] * len(offsets)
    if last:
        operands += [shards[o] for o in range(WINDOW + 1)]
        specs += [ANY] * (WINDOW + 1)
    if not first:
        operands += list(sums[:2])
        specs += [VMEM, VMEM]
    scratch = [
        pltpu.VMEM((ROWS, ROWS), f32),
        pltpu.VMEM((max(1, len(offsets)), 2 * ROWS, HEAD_DIM), bf16),
        pltpu.SemaphoreType.DMA((max(1, len(offsets)),)),
    ]
    aliases = {}
    if last:
        out_shape = jax.ShapeDtypeStruct(wide, bf16)
        out_specs = VMEM
    else:
        out_shape = [jax.ShapeDtypeStruct(wide, f32)] * 2
        if first:
            out_shape.append(jax.ShapeDtypeStruct(wide, bf16))
        else:
            aliases = {len(operands) - 2: 0, len(operands) - 1: 1}
        out_specs = [VMEM] * len(out_shape)
    result = pl.pallas_call(
        functools.partial(attend_kernel, tuple(offsets), own, first, last),
        input_output_aliases=aliases,
        in_specs=specs,
        out_specs=out_specs,
        out_shape=out_shape,
        scratch_shapes=scratch,
        compiler_params=pltpu.CompilerParams(vmem_limit_bytes=20 * 2**20),
        cost_estimate=LIGHT,
        name=name,
    )(*operands)
    if last or first:
        return result
    return [*result, sums[2]]


def rotate(a, distance):
    return lax.ppermute(a, "ctx", [(c, (c + distance) % 16) for c in range(16)])


def turn(a, distance):
    return lax.ppermute(
        a, "ctx", [(4 * x + y, 4 * x + (y + distance) % 4) for x in range(4) for y in range(4)]
    )


def head_swap(a, bit):
    return lax.ppermute(a, "head", [(i, i ^ bit) for i in range(8)])


def after(a, *others):
    return lax.optimization_barrier((a, *others))[0]


def body(
    lin_query, lin_key, lin_value, lin_gate, norm_gain, soft_query, soft_key, soft_value, doc_lengths
):
    place = jnp.reshape(lax.axis_index("ctx"), (1,))
    y = lax.axis_index("ctx") % 4
    gain = norm_gain.reshape(1, -1)

    def behind(distance, here, there):
        return turn(jnp.where(y >= 4 - distance, there, here), distance)

    def attend(place, sums, own, offsets, last, name):
        return attend_call(place, doc_lengths, soft_query, shards, sums, own, offsets, last, name)

    own = jnp.concatenate([soft_key, soft_value], axis=0)
    shards = {0: own}
    shards[4] = rotate(own, 4)
    shards[8] = rotate(own, 8)

    raw, state = linear_call(after(place, own), doc_lengths, lin_query, lin_key, lin_value)
    state_before = rotate(state, 4)
    for k in (1, 3, 2):
        shards[k] = behind(k, after(own, state), shards[4])
    sums = attend(after(place, state), None, True, (4,), False, "attend_a")

    pair = join_call(4, after(place, sums[1]), doc_lengths, state, state_before)
    pair_before = rotate(pair, 1)
    for k in (1, 3, 2):
        shards[k + 4] = behind(k, after(shards[4], pair), shards[8])
    sums = attend(after(place, pair), sums, False, (8, 1), False, "attend_b")

    four = join_call(1, after(place, sums[1]), doc_lengths, pair, pair_before)
    near, far = rotate(four, 1), rotate(four, 3)
    sums = attend(after(place, four), sums, False, (3, 2), False, "attend_c")

    raw, square = inter_call(after(place, sums[1]), doc_lengths, lin_query, near, far, raw)
    for bit in (1, 2):
        square = square + head_swap(square, bit)
    soft_out = attend(after(place, square), sums, False, (5, 7, 6), True, "attend_d")
    lin_out = norm_call(raw, lin_gate, gain, square, head_swap(square, 4))
    return lin_out, soft_out


def solution(mesh):
    split = P("ctx", "head")
    return jax.shard_map(
        body,
        mesh=mesh,
        in_specs=(split, split, split, split, P("head"), split, split, split, P()),
        out_specs=(split, split),
        check_vma=False,
    )
```

```python
import functools

import jax
import jax.numpy as jnp
from jax import lax
from jax.experimental import pallas as pl
from jax.experimental.pallas import tpu as pltpu
from jax.sharding import PartitionSpec as P

HEADS = 64
HEAD_DIM = 128
DOCS = 8
EPS = 1e-06
ROWS = 512
LOCAL = 8
WINDOW = 8
FAR = -1.0e4
SCALE = HEAD_DIM**-0.5 * 1.4426950408889634
f32, bf16, i32 = jnp.float32, jnp.bfloat16, jnp.int32

SMEM = pl.BlockSpec(memory_space=pltpu.SMEM)
VMEM = pl.BlockSpec(memory_space=pltpu.VMEM)
ANY = pl.BlockSpec(memory_space=pl.ANY)
LIGHT = pl.CostEstimate(flops=10**6, bytes_accessed=2**16, transcendentals=0)
SMALL = pltpu.CompilerParams(vmem_limit_bytes=16 * 2**20)


def doc_starts(lens):
    starts = [jnp.int32(0)]
    for d in range(DOCS - 1):
        starts.append(starts[-1] + lens[d])
    return starts


def start_of(starts, pos):
    at = starts[0]
    for s in starts[1:]:
        at = jnp.where(pos >= s, s, at)
    return at


def end_of(starts, pos):
    at = jnp.int32(2**30)
    for s in reversed(starts[1:]):
        at = jnp.where(pos < s, s, at)
    return at


def first_row():
    return lax.axis_index("ctx") * ROWS


def dot_nt(a, b):
    return lax.dot_general(a, b, (((1,), (1,)), ((), ())), preferred_element_type=f32)


def dot_tn(a, b):
    return lax.dot_general(a, b, (((0,), (0,)), ((), ())), preferred_element_type=f32)


def head_cols(h):
    return slice(h * HEAD_DIM, (h + 1) * HEAD_DIM)


def linear_kernel(place, lens, q_ref, k_ref, v_ref, raw_ref, state_ref, mask):
    row0 = place[0] * ROWS
    starts = doc_starts(lens)

    @pl.when(pl.program_id(0) == 0)
    def _():
        rows = lax.broadcasted_iota(i32, (ROWS, ROWS), 0)
        cols = lax.broadcasted_iota(i32, (ROWS, ROWS), 1)
        pos = row0 + lax.broadcasted_iota(i32, (ROWS, 1), 0)
        begin = start_of(starts, pos) - row0
        mask[...] = jnp.where((cols <= rows) & (cols >= begin), 1.0, 0.0).astype(bf16)

    last_begin = start_of(starts, row0 + ROWS - 1) - row0
    keep = lax.broadcasted_iota(i32, (HEAD_DIM, ROWS), 1) >= last_begin
    keep = jnp.where(keep, 1.0, 0.0).astype(bf16)
    half = ROWS // 2
    for h in range(q_ref.shape[1] // HEAD_DIM):
        c = head_cols(h)
        state_ref[c, :] = jnp.dot(
            k_ref[:, c].T * keep, v_ref[:, c], preferred_element_type=f32
        ).astype(bf16)
        for r, width in ((0, half), (half, ROWS)):
            rows = slice(r, r + half)
            s = dot_nt(q_ref[rows, c], k_ref[:width, c]).astype(bf16) * mask[rows, :width]
            raw_ref[rows, c] = jnp.dot(s, v_ref[:width, c], preferred_element_type=f32)


def linear_call(place, lens, q, k, v):
    step = 4 * HEAD_DIM
    block = pl.BlockSpec((ROWS, step), lambda g: (0, g))
    return pl.pallas_call(
        linear_kernel,
        grid=(LOCAL * HEAD_DIM // step,),
        in_specs=[SMEM, SMEM, block, block, block],
        out_specs=(block, pl.BlockSpec((step, HEAD_DIM), lambda g: (g, 0))),
        out_shape=(
            jax.ShapeDtypeStruct((ROWS, LOCAL * HEAD_DIM), f32),
            jax.ShapeDtypeStruct((LOCAL * HEAD_DIM, HEAD_DIM), bf16),
        ),
        scratch_shapes=[pltpu.VMEM((ROWS, ROWS), bf16)],
        cost_estimate=LIGHT,
        name="linear",
    )(place, lens, q, k, v)


def join_kernel(distance, place, lens, own_ref, got_ref, out_ref):
    row0 = place[0] * ROWS
    same = start_of(doc_starts(lens), row0 + ROWS - 1) < row0 - (distance - 1) * ROWS
    take = jnp.where(same & (place[0] >= distance), 1.0, 0.0)
    out_ref[...] = (own_ref[...].astype(f32) + take * got_ref[...].astype(f32)).astype(bf16)


def join_call(distance, place, lens, own, got):
    return pl.pallas_call(
        functools.partial(join_kernel, distance),
        in_specs=[SMEM, SMEM, VMEM, VMEM],
        out_specs=VMEM,
        out_shape=jax.ShapeDtypeStruct(own.shape, bf16),
        compiler_params=SMALL,
        cost_estimate=LIGHT,
        name=f"join{distance}",
    )(place, lens, own, got)


def inter_kernel(place, lens, q_ref, near_ref, far_ref, raw_ref, out_ref, square_ref):
    row0 = place[0] * ROWS
    starts = doc_starts(lens)
    reach = jnp.where(place[0] > 0, end_of(starts, row0 - 1) - row0, 0)
    inside = lax.broadcasted_iota(i32, (ROWS, HEAD_DIM), 0) < reach
    take = jnp.where(
        (start_of(starts, row0 - 1) < row0 - 2 * ROWS) & (place[0] >= 3), 1.0, 0.0
    )
    squares = jnp.zeros((ROWS, HEAD_DIM), f32)
    for h in range(LOCAL):
        c = head_cols(h)
        state = (near_ref[c, :].astype(f32) + take * far_ref[c, :].astype(f32)).astype(bf16)
        carried = jnp.dot(q_ref[:, c], state, preferred_element_type=f32)
        raw = raw_ref[:, c] + jnp.where(inside, carried, 0.0)
        out_ref[:, c] = raw
        squares = squares + raw * raw
    ones = jnp.ones((8, HEAD_DIM), f32)
    square_ref[...] = lax.dot_general(
        ones, squares, (((1,), (1,)), ((), ())), precision=lax.Precision.HIGHEST,
        preferred_element_type=f32,
    )


def inter_call(place, lens, q, near, far, raw):
    return pl.pallas_call(
        inter_kernel,
        in_specs=[SMEM, SMEM] + [VMEM] * 4,
        out_specs=(VMEM, VMEM),
        out_shape=(
            jax.ShapeDtypeStruct(raw.shape, f32),
            jax.ShapeDtypeStruct((8, ROWS), f32),
        ),
        input_output_aliases={5: 0},
        compiler_params=SMALL,
        cost_estimate=LIGHT,
        name="inter",
    )(place, lens, q, near, far, raw)


def norm_kernel(raw_ref, gate_ref, gain_ref, near_ref, far_ref, out_ref, inverse):
    @pl.when(pl.program_id(0) == 0)
    def _():
        ones = jnp.full((8, HEAD_DIM), 0.125, f32)
        total = lax.dot_general(
            near_ref[...] + far_ref[...], ones, (((0,), (0,)), ((), ())),
            precision=lax.Precision.HIGHEST, preferred_element_type=f32,
        )
        inverse[...] = lax.rsqrt(total / (HEADS * HEAD_DIM) + EPS)

    for h in range(raw_ref.shape[1] // HEAD_DIM):
        c = head_cols(h)
        gate = jax.nn.sigmoid(gate_ref[:, c].astype(f32))
        out_ref[:, c] = (raw_ref[:, c] * inverse[...] * gain_ref[:, c] * gate).astype(bf16)


def norm_call(raw, gate, gain, near, far):
    step = 4 * HEAD_DIM
    block = pl.BlockSpec((ROWS, step), lambda g: (0, g))
    square = pl.BlockSpec((8, ROWS), lambda g: (0, 0))
    return pl.pallas_call(
        norm_kernel,
        grid=(LOCAL * HEAD_DIM // step,),
        in_specs=[block, block, pl.BlockSpec((1, step), lambda g: (0, g)), square, square],
        out_specs=block,
        out_shape=jax.ShapeDtypeStruct((ROWS, LOCAL * HEAD_DIM), bf16),
        scratch_shapes=[pltpu.VMEM((ROWS, HEAD_DIM), f32)],
        compiler_params=SMALL,
        cost_estimate=LIGHT,
        name="norm",
    )(raw, gate, gain, near, far)


def attend_kernel(offsets, own, first, last, *refs):
    refs = list(refs)
    place, lens, q_ref = refs[:3]
    del refs[:3]
    count = len(offsets)
    every = tuple(range(WINDOW + 1)) if last else ()
    own_ref = refs.pop(0) if own else None
    shard_refs = [refs.pop(0) for _ in offsets]
    every_refs = [refs.pop(0) for _ in every]
    if not first:
        acc, part = refs.pop(0), refs.pop(0)
    if last:
        out_ref = refs.pop(0)
    else:
        acc, part = refs.pop(0), refs.pop(0)
    if first:
        queries = refs.pop(0)
    else:
        queries = q_ref
    bias, held, sems = refs

    row0 = place[0] * ROWS
    starts = doc_starts(lens)
    first_start, last_start = start_of(starts, row0), start_of(starts, row0 + ROWS - 1)

    def needed(offset):
        begin = row0 - offset * ROWS
        return (begin >= 0) & (first_start < begin + ROWS)

    def copy(ref, slot):
        return pltpu.make_async_copy(ref, held.at[slot], sems.at[slot])

    for slot, offset in enumerate(offsets):

        @pl.when(needed(offset))
        def _(slot=slot):
            copy(shard_refs[slot], slot).start()

    if first:
        queries[...] = (q_ref[...].astype(f32) * SCALE).astype(bf16)
        part[...] = jnp.zeros_like(part)
        acc[...] = jnp.zeros_like(acc)

    def set_bias(offset, causal):
        pos = row0 + lax.broadcasted_iota(i32, (ROWS, 1), 0)
        begin = start_of(starts, pos)
        keys = row0 - offset * ROWS + lax.broadcasted_iota(i32, (ROWS, ROWS), 1)
        allowed = keys >= begin
        if causal:
            allowed = allowed & (keys <= row0 + lax.broadcasted_iota(i32, (ROWS, ROWS), 0))
        bias[...] = jnp.where(allowed, 0.0, FAR)

    def add(rows, c, keys, values, width, masked):
        s = dot_nt(queries[rows, c], keys)
        if masked:
            s = s + bias[rows, :width]
        p = jnp.exp2(s)
        acc[rows, c] += jnp.dot(p.astype(bf16), values, preferred_element_type=f32)
        sums = p[:, :HEAD_DIM]
        for at in range(HEAD_DIM, width, HEAD_DIM):
            sums = sums + p[:, at : at + HEAD_DIM]
        part[rows, c] += sums

    if own:
        set_bias(0, True)
        half = ROWS // 2
        for h in range(LOCAL):
            for r, width in ((0, half), (half, ROWS)):
                rows = slice(r, r + half)
                add(rows, head_cols(h), own_ref[:width, :], own_ref[ROWS : ROWS + width, :], width, True)

    def one(slot, _):
        offset = jnp.int32(offsets[0])
        for i in range(1, count):
            offset = jnp.where(slot == i, offsets[i], offset)
        use = needed(offset)
        free = last_start <= row0 - offset * ROWS

        def every_head(masked):
            for h in range(LOCAL):
                add(slice(None), head_cols(h), held[slot, :ROWS, :], held[slot, ROWS:, :], ROWS, masked)

        @pl.when(use)
        def _():
            copy(shard_refs[0], slot).wait()

        @pl.when(use)
        def _():
            @pl.when(free)
            def _():
                bias[...] = jnp.zeros_like(bias)

            @pl.when(jnp.logical_not(free))
            def _():
                set_bias(offset, False)

            every_head(True)

        return 0

    if count:
        lax.fori_loop(0, count, one, 0)
    if not last:
        return

    low = high = jnp.ones((ROWS, 1), f32)
    for h in range(LOCAL):
        c = head_cols(h)
        total = jnp.sum(part[:, c], axis=1, keepdims=True)
        low, high = jnp.minimum(low, total), jnp.maximum(high, total)
        out_ref[:, c] = (acc[:, c] / total).astype(bf16)

    @pl.when((jnp.min(low) < 2.0**-60) | (jnp.max(high) > 2.0**100))
    def _():
        lane = lax.broadcasted_iota(i32, (ROWS, HEAD_DIM), 1)
        acc[...] = jnp.zeros_like(acc)
        for h in range(LOCAL):
            part[:, head_cols(h)] = jnp.where(lane == 0, -1.0e30, 0.0)
        def again(offset, _):
            for k in every:

                @pl.when(offset == k)
                def _(k=k):
                    fetch = pltpu.make_async_copy(every_refs[k], held.at[0], sems.at[0])
                    fetch.start()
                    fetch.wait()

            set_bias(offset, True)

            def one_head(h, _):
                c = pl.ds(pl.multiple_of(h * HEAD_DIM, HEAD_DIM), HEAD_DIM)
                s = dot_nt(queries[:, c], held[0, :ROWS, :]) + bias[...]
                old = part[:, c]
                peak, gone = old[:, 0:1], old[:, 1:2]
                new = jnp.maximum(peak, jnp.max(s, axis=1, keepdims=True))
                p = jnp.exp2(s - new)
                shrink = jnp.exp2(peak - new)
                acc[:, c] = acc[:, c] * shrink + jnp.dot(
                    p.astype(bf16), held[0, ROWS:, :], preferred_element_type=f32
                )
                gone = gone * shrink + jnp.sum(p, axis=1, keepdims=True)
                part[:, c] = jnp.where(lane == 0, new, gone)
                return 0

            lax.fori_loop(0, LOCAL, one_head, 0)
            return 0

        lax.fori_loop(0, jnp.minimum(place[0], WINDOW) + 1, again, 0)
        for h in range(LOCAL):
            c = head_cols(h)
            out_ref[:, c] = (acc[:, c] / part[:, c][:, 1:2]).astype(bf16)


def attend_call(place, lens, q, shards, sums, own, offsets, last, name):
    first = sums is None
    wide = q.shape
    operands, specs = [place, lens, q if first else sums[2]], [SMEM, SMEM, VMEM]
    if own:
        operands.append(shards[0])
        specs.append(VMEM)
    operands += [shards[o] for o in offsets]
    specs += [ANY] * len(offsets)
    if last:
        operands += [shards[o] for o in range(WINDOW + 1)]
        specs += [ANY] * (WINDOW + 1)
    if not first:
        operands += list(sums[:2])
        specs += [VMEM, VMEM]
    scratch = [
        pltpu.VMEM((ROWS, ROWS), f32),
        pltpu.VMEM((max(1, len(offsets)), 2 * ROWS, HEAD_DIM), bf16),
        pltpu.SemaphoreType.DMA((max(1, len(offsets)),)),
    ]
    aliases = {}
    if last:
        out_shape = jax.ShapeDtypeStruct(wide, bf16)
        out_specs = VMEM
    else:
        out_shape = [jax.ShapeDtypeStruct(wide, f32)] * 2
        if first:
            out_shape.append(jax.ShapeDtypeStruct(wide, bf16))
        else:
            aliases = {len(operands) - 2: 0, len(operands) - 1: 1}
        out_specs = [VMEM] * len(out_shape)
    result = pl.pallas_call(
        functools.partial(attend_kernel, tuple(offsets), own, first, last),
        input_output_aliases=aliases,
        in_specs=specs,
        out_specs=out_specs,
        out_shape=out_shape,
        scratch_shapes=scratch,
        compiler_params=pltpu.CompilerParams(vmem_limit_bytes=20 * 2**20),
        cost_estimate=LIGHT,
        name=name,
    )(*operands)
    if last or first:
        return result
    return [*result, sums[2]]


def rotate(a, distance):
    return lax.ppermute(a, "ctx", [(c, (c + distance) % 16) for c in range(16)])


def turn(a, distance):
    return lax.ppermute(
        a, "ctx", [(4 * x + y, 4 * x + (y + distance) % 4) for x in range(4) for y in range(4)]
    )


def head_swap(a, bit):
    return lax.ppermute(a, "head", [(i, i ^ bit) for i in range(8)])


def after(a, *others):
    return lax.optimization_barrier((a, *others))[0]


def body(
    lin_query, lin_key, lin_value, lin_gate, norm_gain, soft_query, soft_key, soft_value, doc_lengths
):
    place = jnp.reshape(lax.axis_index("ctx"), (1,))
    y = lax.axis_index("ctx") % 4
    gain = norm_gain.reshape(1, -1)

    def behind(distance, here, there):
        return turn(jnp.where(y >= 4 - distance, there, here), distance)

    def attend(place, sums, own, offsets, last, name):
        return attend_call(place, doc_lengths, soft_query, shards, sums, own, offsets, last, name)

    own = jnp.concatenate([soft_key, soft_value], axis=0)
    shards = {0: own}
    shards[4] = rotate(own, 4)
    shards[8] = rotate(own, 8)

    raw, state = linear_call(after(place, own), doc_lengths, lin_query, lin_key, lin_value)
    state_before = rotate(state, 4)
    for k in (1, 3, 2):
        shards[k] = behind(k, after(own, state), shards[4])
    sums = attend(after(place, state), None, True, (4,), False, "attend_a")

    pair = join_call(4, after(place, sums[1]), doc_lengths, state, state_before)
    pair_before = rotate(pair, 1)
    for k in (1, 3):
        shards[k + 4] = behind(k, after(shards[4], pair), shards[8])
    shards[6] = rotate(after(shards[2], pair), 4)
    sums = attend(after(place, pair), sums, False, (8, 1, 3), False, "attend_b")

    four = join_call(1, after(place, sums[1]), doc_lengths, pair, pair_before)
    near, far = rotate(four, 1), rotate(four, 3)
    sums = attend(after(place, four), sums, False, (2,), False, "attend_c")

    raw, square = inter_call(after(place, sums[1]), doc_lengths, lin_query, near, far, raw)
    for bit in (1, 2):
        square = square + head_swap(square, bit)
    soft_out = attend(after(place, square), sums, False, (5, 7, 6), True, "attend_d")
    lin_out = norm_call(raw, lin_gate, gain, square, head_swap(square, 4))
    return lin_out, soft_out


def solution(mesh):
    split = P("ctx", "head")
    return jax.shard_map(
        body,
        mesh=mesh,
        in_specs=(split, split, split, split, P("head"), split, split, split, P()),
        out_specs=(split, split),
        check_vma=False,
    )
```

```python
import functools

import jax
import jax.numpy as jnp
from jax import lax
from jax.experimental import pallas as pl
from jax.experimental.pallas import tpu as pltpu
from jax.sharding import PartitionSpec as P

HEADS = 64
HEAD_DIM = 128
DOCS = 8
EPS = 1e-06
ROWS = 512
LOCAL = 8
WINDOW = 8
FAR = -1.0e4
SCALE = HEAD_DIM**-0.5 * 1.4426950408889634
f32, bf16, i32 = jnp.float32, jnp.bfloat16, jnp.int32

SMEM = pl.BlockSpec(memory_space=pltpu.SMEM)
VMEM = pl.BlockSpec(memory_space=pltpu.VMEM)
ANY = pl.BlockSpec(memory_space=pl.ANY)
LIGHT = pl.CostEstimate(flops=10**6, bytes_accessed=2**16, transcendentals=0)
SMALL = pltpu.CompilerParams(vmem_limit_bytes=16 * 2**20)


def doc_starts(lens):
    starts = [jnp.int32(0)]
    for d in range(DOCS - 1):
        starts.append(starts[-1] + lens[d])
    return starts


def start_of(starts, pos):
    at = starts[0]
    for s in starts[1:]:
        at = jnp.where(pos >= s, s, at)
    return at


def end_of(starts, pos):
    at = jnp.int32(2**30)
    for s in reversed(starts[1:]):
        at = jnp.where(pos < s, s, at)
    return at


def first_row():
    return lax.axis_index("ctx") * ROWS


def dot_nt(a, b):
    return lax.dot_general(a, b, (((1,), (1,)), ((), ())), preferred_element_type=f32)


def dot_tn(a, b):
    return lax.dot_general(a, b, (((0,), (0,)), ((), ())), preferred_element_type=f32)


def head_cols(h):
    return slice(h * HEAD_DIM, (h + 1) * HEAD_DIM)


def linear_kernel(place, lens, q_ref, k_ref, v_ref, raw_ref, state_ref, mask):
    row0 = place[0] * ROWS
    starts = doc_starts(lens)

    @pl.when(pl.program_id(0) == 0)
    def _():
        rows = lax.broadcasted_iota(i32, (ROWS, ROWS), 0)
        cols = lax.broadcasted_iota(i32, (ROWS, ROWS), 1)
        pos = row0 + lax.broadcasted_iota(i32, (ROWS, 1), 0)
        begin = start_of(starts, pos) - row0
        mask[...] = jnp.where((cols <= rows) & (cols >= begin), 1.0, 0.0).astype(bf16)

    last_begin = start_of(starts, row0 + ROWS - 1) - row0
    keep = lax.broadcasted_iota(i32, (HEAD_DIM, ROWS), 1) >= last_begin
    keep = jnp.where(keep, 1.0, 0.0).astype(bf16)
    half = ROWS // 2
    for h in range(q_ref.shape[1] // HEAD_DIM):
        c = head_cols(h)
        state_ref[c, :] = jnp.dot(
            k_ref[:, c].T * keep, v_ref[:, c], preferred_element_type=f32
        ).astype(bf16)
        for r, width in ((0, half), (half, ROWS)):
            rows = slice(r, r + half)
            s = dot_nt(q_ref[rows, c], k_ref[:width, c]).astype(bf16) * mask[rows, :width]
            raw_ref[rows, c] = jnp.dot(s, v_ref[:width, c], preferred_element_type=f32)


def linear_call(place, lens, q, k, v):
    step = 4 * HEAD_DIM
    block = pl.BlockSpec((ROWS, step), lambda g: (0, g))
    return pl.pallas_call(
        linear_kernel,
        grid=(LOCAL * HEAD_DIM // step,),
        in_specs=[SMEM, SMEM, block, block, block],
        out_specs=(block, pl.BlockSpec((step, HEAD_DIM), lambda g: (g, 0))),
        out_shape=(
            jax.ShapeDtypeStruct((ROWS, LOCAL * HEAD_DIM), f32),
            jax.ShapeDtypeStruct((LOCAL * HEAD_DIM, HEAD_DIM), bf16),
        ),
        scratch_shapes=[pltpu.VMEM((ROWS, ROWS), bf16)],
        cost_estimate=LIGHT,
        name="linear",
    )(place, lens, q, k, v)


def join_kernel(distance, place, lens, own_ref, got_ref, out_ref):
    row0 = place[0] * ROWS
    same = start_of(doc_starts(lens), row0 + ROWS - 1) < row0 - (distance - 1) * ROWS
    take = jnp.where(same & (place[0] >= distance), 1.0, 0.0)
    out_ref[...] = (own_ref[...].astype(f32) + take * got_ref[...].astype(f32)).astype(bf16)


def join_call(distance, place, lens, own, got):
    return pl.pallas_call(
        functools.partial(join_kernel, distance),
        in_specs=[SMEM, SMEM, VMEM, VMEM],
        out_specs=VMEM,
        out_shape=jax.ShapeDtypeStruct(own.shape, bf16),
        compiler_params=SMALL,
        cost_estimate=LIGHT,
        name=f"join{distance}",
    )(place, lens, own, got)


def inter_kernel(place, lens, q_ref, near_ref, far_ref, raw_ref, out_ref, square_ref):
    row0 = place[0] * ROWS
    starts = doc_starts(lens)
    reach = jnp.where(place[0] > 0, end_of(starts, row0 - 1) - row0, 0)
    inside = lax.broadcasted_iota(i32, (ROWS, HEAD_DIM), 0) < reach
    take = jnp.where(
        (start_of(starts, row0 - 1) < row0 - 2 * ROWS) & (place[0] >= 3), 1.0, 0.0
    )
    squares = jnp.zeros((ROWS, HEAD_DIM), f32)
    for h in range(LOCAL):
        c = head_cols(h)
        state = (near_ref[c, :].astype(f32) + take * far_ref[c, :].astype(f32)).astype(bf16)
        carried = jnp.dot(q_ref[:, c], state, preferred_element_type=f32)
        raw = raw_ref[:, c] + jnp.where(inside, carried, 0.0)
        out_ref[:, c] = raw
        squares = squares + raw * raw
    ones = jnp.ones((8, HEAD_DIM), f32)
    square_ref[...] = lax.dot_general(
        ones, squares, (((1,), (1,)), ((), ())), precision=lax.Precision.HIGHEST,
        preferred_element_type=f32,
    )


def inter_call(place, lens, q, near, far, raw):
    return pl.pallas_call(
        inter_kernel,
        in_specs=[SMEM, SMEM] + [VMEM] * 4,
        out_specs=(VMEM, VMEM),
        out_shape=(
            jax.ShapeDtypeStruct(raw.shape, f32),
            jax.ShapeDtypeStruct((8, ROWS), f32),
        ),
        input_output_aliases={5: 0},
        compiler_params=SMALL,
        cost_estimate=LIGHT,
        name="inter",
    )(place, lens, q, near, far, raw)


def norm_kernel(raw_ref, gate_ref, gain_ref, near_ref, far_ref, out_ref, inverse):
    @pl.when(pl.program_id(0) == 0)
    def _():
        ones = jnp.full((8, HEAD_DIM), 0.125, f32)
        total = lax.dot_general(
            near_ref[...] + far_ref[...], ones, (((0,), (0,)), ((), ())),
            precision=lax.Precision.HIGHEST, preferred_element_type=f32,
        )
        inverse[...] = lax.rsqrt(total / (HEADS * HEAD_DIM) + EPS)

    for h in range(raw_ref.shape[1] // HEAD_DIM):
        c = head_cols(h)
        gate = jax.nn.sigmoid(gate_ref[:, c].astype(f32))
        out_ref[:, c] = (raw_ref[:, c] * inverse[...] * gain_ref[:, c] * gate).astype(bf16)


def norm_call(raw, gate, gain, near, far):
    step = 4 * HEAD_DIM
    block = pl.BlockSpec((ROWS, step), lambda g: (0, g))
    square = pl.BlockSpec((8, ROWS), lambda g: (0, 0))
    return pl.pallas_call(
        norm_kernel,
        grid=(LOCAL * HEAD_DIM // step,),
        in_specs=[block, block, pl.BlockSpec((1, step), lambda g: (0, g)), square, square],
        out_specs=block,
        out_shape=jax.ShapeDtypeStruct((ROWS, LOCAL * HEAD_DIM), bf16),
        scratch_shapes=[pltpu.VMEM((ROWS, HEAD_DIM), f32)],
        compiler_params=SMALL,
        cost_estimate=LIGHT,
        name="norm",
    )(raw, gate, gain, near, far)


def attend_kernel(offsets, own, first, last, *refs):
    refs = list(refs)
    place, lens, q_ref = refs[:3]
    del refs[:3]
    count = len(offsets)
    every = tuple(range(WINDOW + 1)) if last else ()
    own_ref = refs.pop(0) if own else None
    shard_refs = [refs.pop(0) for _ in offsets]
    every_refs = [refs.pop(0) for _ in every]
    if not first:
        acc, part = refs.pop(0), refs.pop(0)
    if last:
        out_ref = refs.pop(0)
    else:
        acc, part = refs.pop(0), refs.pop(0)
    if first:
        queries = refs.pop(0)
    else:
        queries = q_ref
    edge, bias, held, sems = refs

    row0 = place[0] * ROWS
    starts = doc_starts(lens)
    first_start, last_start = start_of(starts, row0), start_of(starts, row0 + ROWS - 1)

    def needed(offset):
        begin = row0 - offset * ROWS
        return (begin >= 0) & (first_start < begin + ROWS)

    def copy(ref, slot):
        return pltpu.make_async_copy(ref, held.at[slot], sems.at[slot])

    for slot, offset in enumerate(offsets):

        @pl.when(needed(offset))
        def _(slot=slot):
            copy(shard_refs[slot], slot).start()

    if first:
        queries[...] = (q_ref[...].astype(f32) * SCALE).astype(bf16)
        part[...] = jnp.zeros_like(part)
        acc[...] = jnp.zeros_like(acc)

    def set_edge():
        pos = row0 + lax.broadcasted_iota(i32, (ROWS, 1), 0)
        edge[...] = start_of(starts, pos) - row0 - lax.broadcasted_iota(i32, (ROWS, ROWS), 1)

    def set_bias(offset, causal):
        allowed = edge[...] <= -offset * ROWS
        if causal:
            rows = lax.broadcasted_iota(i32, (ROWS, ROWS), 0) + offset * ROWS
            allowed = allowed & (lax.broadcasted_iota(i32, (ROWS, ROWS), 1) <= rows)
        bias[...] = jnp.where(allowed, 0.0, FAR)

    if own:
        set_edge()
    else:

        @pl.when(last_start > row0 - max(offsets) * ROWS)
        def _():
            set_edge()

    def add(rows, c, keys, values, width, masked):
        s = dot_nt(queries[rows, c], keys)
        if masked:
            s = s + bias[rows, :width]
        p = jnp.exp2(s)
        acc[rows, c] += jnp.dot(p.astype(bf16), values, preferred_element_type=f32)
        sums = p[:, :HEAD_DIM]
        for at in range(HEAD_DIM, width, HEAD_DIM):
            sums = sums + p[:, at : at + HEAD_DIM]
        part[rows, c] += sums

    if own:
        set_bias(0, True)
        half = ROWS // 2
        for h in range(LOCAL):
            for r, width in ((0, half), (half, ROWS)):
                rows = slice(r, r + half)
                add(rows, head_cols(h), own_ref[:width, :], own_ref[ROWS : ROWS + width, :], width, True)

    def one(slot, _):
        offset = jnp.int32(offsets[0])
        for i in range(1, count):
            offset = jnp.where(slot == i, offsets[i], offset)
        use = needed(offset)
        free = last_start <= row0 - offset * ROWS

        def every_head(masked):
            for h in range(LOCAL):
                add(slice(None), head_cols(h), held[slot, :ROWS, :], held[slot, ROWS:, :], ROWS, masked)

        @pl.when(use)
        def _():
            copy(shard_refs[0], slot).wait()

        @pl.when(use)
        def _():
            @pl.when(free)
            def _():
                bias[...] = jnp.zeros_like(bias)

            @pl.when(jnp.logical_not(free))
            def _():
                set_bias(offset, False)

            every_head(True)

        return 0

    if count:
        lax.fori_loop(0, count, one, 0)
    if not last:
        return

    low = high = jnp.ones((ROWS, 1), f32)
    for h in range(LOCAL):
        c = head_cols(h)
        total = jnp.sum(part[:, c], axis=1, keepdims=True)
        low, high = jnp.minimum(low, total), jnp.maximum(high, total)
        out_ref[:, c] = (acc[:, c] / total).astype(bf16)

    @pl.when((jnp.min(low) < 2.0**-60) | (jnp.max(high) > 2.0**100))
    def _():
        lane = lax.broadcasted_iota(i32, (ROWS, HEAD_DIM), 1)
        set_edge()
        acc[...] = jnp.zeros_like(acc)
        for h in range(LOCAL):
            part[:, head_cols(h)] = jnp.where(lane == 0, -1.0e30, 0.0)
        def again(offset, _):
            for k in every:

                @pl.when(offset == k)
                def _(k=k):
                    fetch = pltpu.make_async_copy(every_refs[k], held.at[0], sems.at[0])
                    fetch.start()
                    fetch.wait()

            set_bias(offset, True)

            def one_head(h, _):
                c = pl.ds(pl.multiple_of(h * HEAD_DIM, HEAD_DIM), HEAD_DIM)
                s = dot_nt(queries[:, c], held[0, :ROWS, :]) + bias[...]
                old = part[:, c]
                peak, gone = old[:, 0:1], old[:, 1:2]
                new = jnp.maximum(peak, jnp.max(s, axis=1, keepdims=True))
                p = jnp.exp2(s - new)
                shrink = jnp.exp2(peak - new)
                acc[:, c] = acc[:, c] * shrink + jnp.dot(
                    p.astype(bf16), held[0, ROWS:, :], preferred_element_type=f32
                )
                gone = gone * shrink + jnp.sum(p, axis=1, keepdims=True)
                part[:, c] = jnp.where(lane == 0, new, gone)
                return 0

            lax.fori_loop(0, LOCAL, one_head, 0)
            return 0

        lax.fori_loop(0, jnp.minimum(place[0], WINDOW) + 1, again, 0)
        for h in range(LOCAL):
            c = head_cols(h)
            out_ref[:, c] = (acc[:, c] / part[:, c][:, 1:2]).astype(bf16)


def attend_call(place, lens, q, shards, sums, own, offsets, last, name):
    first = sums is None
    wide = q.shape
    operands, specs = [place, lens, q if first else sums[2]], [SMEM, SMEM, VMEM]
    if own:
        operands.append(shards[0])
        specs.append(VMEM)
    operands += [shards[o] for o in offsets]
    specs += [ANY] * len(offsets)
    if last:
        operands += [shards[o] for o in range(WINDOW + 1)]
        specs += [ANY] * (WINDOW + 1)
    if not first:
        operands += list(sums[:2])
        specs += [VMEM, VMEM]
    scratch = [
        pltpu.VMEM((ROWS, ROWS), i32),
        pltpu.VMEM((ROWS, ROWS), f32),
        pltpu.VMEM((max(1, len(offsets)), 2 * ROWS, HEAD_DIM), bf16),
        pltpu.SemaphoreType.DMA((max(1, len(offsets)),)),
    ]
    aliases = {}
    if last:
        out_shape = jax.ShapeDtypeStruct(wide, bf16)
        out_specs = VMEM
    else:
        out_shape = [jax.ShapeDtypeStruct(wide, f32)] * 2
        if first:
            out_shape.append(jax.ShapeDtypeStruct(wide, bf16))
        else:
            aliases = {len(operands) - 2: 0, len(operands) - 1: 1}
        out_specs = [VMEM] * len(out_shape)
    result = pl.pallas_call(
        functools.partial(attend_kernel, tuple(offsets), own, first, last),
        input_output_aliases=aliases,
        in_specs=specs,
        out_specs=out_specs,
        out_shape=out_shape,
        scratch_shapes=scratch,
        compiler_params=pltpu.CompilerParams(vmem_limit_bytes=20 * 2**20),
        cost_estimate=LIGHT,
        name=name,
    )(*operands)
    if last or first:
        return result
    return [*result, sums[2]]


def rotate(a, distance):
    return lax.ppermute(a, "ctx", [(c, (c + distance) % 16) for c in range(16)])


def turn(a, distance):
    return lax.ppermute(
        a, "ctx", [(4 * x + y, 4 * x + (y + distance) % 4) for x in range(4) for y in range(4)]
    )


def head_swap(a, bit):
    return lax.ppermute(a, "head", [(i, i ^ bit) for i in range(8)])


def after(a, *others):
    return lax.optimization_barrier((a, *others))[0]


def body(
    lin_query, lin_key, lin_value, lin_gate, norm_gain, soft_query, soft_key, soft_value, doc_lengths
):
    place = jnp.reshape(lax.axis_index("ctx"), (1,))
    y = lax.axis_index("ctx") % 4
    gain = norm_gain.reshape(1, -1)

    def behind(distance, here, there):
        return turn(jnp.where(y >= 4 - distance, there, here), distance)

    def attend(place, sums, own, offsets, last, name):
        return attend_call(place, doc_lengths, soft_query, shards, sums, own, offsets, last, name)

    own = jnp.concatenate([soft_key, soft_value], axis=0)
    shards = {0: own}
    shards[4] = rotate(own, 4)
    shards[8] = rotate(own, 8)

    raw, state = linear_call(after(place, own), doc_lengths, lin_query, lin_key, lin_value)
    state_before = rotate(state, 4)
    for k in (1, 3, 2):
        shards[k] = behind(k, after(own, state), shards[4])
    sums = attend(after(place, state), None, True, (4,), False, "attend_a")

    pair = join_call(4, after(place, sums[1]), doc_lengths, state, state_before)
    pair_before = rotate(pair, 1)
    for k in (1, 3):
        shards[k + 4] = behind(k, after(shards[4], pair), shards[8])
    shards[6] = rotate(after(shards[2], pair), 4)
    sums = attend(after(place, pair), sums, False, (8, 1, 3), False, "attend_b")

    four = join_call(1, after(place, sums[1]), doc_lengths, pair, pair_before)
    near, far = rotate(four, 1), rotate(four, 3)
    sums = attend(after(place, four), sums, False, (2,), False, "attend_c")

    raw, square = inter_call(after(place, sums[1]), doc_lengths, lin_query, near, far, raw)
    for bit in (1, 2):
        square = square + head_swap(square, bit)
    soft_out = attend(after(place, square), sums, False, (5, 7, 6), True, "attend_d")
    lin_out = norm_call(raw, lin_gate, gain, square, head_swap(square, 4))
    return lin_out, soft_out


def solution(mesh):
    split = P("ctx", "head")
    return jax.shard_map(
        body,
        mesh=mesh,
        in_specs=(split, split, split, split, P("head"), split, split, split, P()),
        out_specs=(split, split),
        check_vma=False,
    )
```
